128 devices in a mesh: pipe: 2 (over x_lo), dp: 64 (over z, y, x_hi, core).
Axes of the slice: x: 4 (x_hi: 2, x_lo: 2; x = x_hi * 2 + x_lo), y: 4, z: 4, core: 2. Of those that a mesh axis runs over, the one named last changes fastest.
Arguments:
- stack_input: bfloat16 [2, 8192, 8192], P(None, 'dp', 'pipe'), may hold values from -6 to 6
- output_gradient: bfloat16 [2, 8192, 8192], P(None, 'dp', 'pipe'), may hold values from -1.5 to 1.5
- norm_scale_weight: float32 [2, 8192], P('pipe'), may hold values from 0.5 to 1.5
- row_adapter_index: int32 [2, 8192, 1], P(None, 'dp'), may hold values from 0 to 63; in each aligned block of 128 rows (0 to 127, 128 to 255, ..., all dimensions but the last counted through in order) at most 4 rows name the same one
- adapter_owner_index: int32 [64], replicated, may hold values from 0 to 63, each once
- adapter_down_weight: bfloat16 [2, 64, 32, 8192], P('pipe', 'dp'), may hold values from -0.0625 to 0.0625
- adapter_up_weight: bfloat16 [2, 64, 32, 8192], P('pipe', 'dp'), may hold values from -1 to 1
- down_first_moment: float32 [2, 64, 32, 8192], P('pipe', 'dp'), may hold values from -12 to 12
- down_second_moment: float32 [2, 64, 32, 8192], P('pipe', 'dp'), may hold values from 1 to 1000
- up_first_moment: float32 [2, 64, 32, 8192], P('pipe', 'dp'), may hold values from -1.2 to 1.2
- up_second_moment: float32 [2, 64, 32, 8192], P('pipe', 'dp'), may hold values from 0.01 to 10
Outputs:
- down_weight_next: bfloat16 [2, 64, 32, 8192], P('pipe', 'dp')
- up_weight_next: bfloat16 [2, 64, 32, 8192], P('pipe', 'dp')
- down_first_moment_next: float32 [2, 64, 32, 8192], P('pipe', 'dp')
- down_second_moment_next: float32 [2, 64, 32, 8192], P('pipe', 'dp')
- up_first_moment_next: float32 [2, 64, 32, 8192], P('pipe', 'dp')
- up_second_moment_next: float32 [2, 64, 32, 8192], P('pipe', 'dp')
The draws below stay inside these ranges and needn't reach their ends.
Inputs may be any that keep to these rules, and one draw needn't show every extreme that they name: `row_adapter_index`: in each micro-batch the 128 rows of one device name any one adapter at most 4 times. Every index of dp owns exactly one adapter; adapter a's projections and moments stand at index adapter_owner_index[a] of their second dimension.
All inputs are finite; a program needn't handle non-finite values.
Results may differ from the reference program's by a relative error of at most 0.0055.
Values may be sent and summed in bfloat16 or wider, within the bound.
A program may use at most 192 MiB of HBM per device.

```python
import math
import jax
import jax.numpy as jnp
import numpy as np
from jax import lax

MODEL_WIDTH = 8192
ADAPTER_RANK = 32
MICRO = 2
TOK_DEV = 128
LAYER_TOTAL = 2
ADAPTER_TOTAL = 64
CAP = 4
TOKENS = 8192
N_DP = 64


def levels(rng, extent, cuts, low, high):
    def one(dim, blocks):
        steps = jax.random.uniform(jax.random.fold_in(jax.random.fold_in(rng, 6), dim), (blocks,), jnp.float32, low / len(cuts), high / len(cuts))
        return jnp.repeat(jnp.exp(steps), extent[dim] // blocks).reshape((-1,) + (1,) * (len(extent) - dim - 1))

    gain = one(*cuts[0])
    for cut in cuts[1:]:
        gain = gain * one(*cut)
    return gain


def deal_out(key, own, number, rows, number_of, top, reach, lean):
    sequence = jax.random.permutation(key, number_of)
    packed, usual = portions_of(number_of, rows * top, reach, lean, True), portions_of(number_of, rows * top, reach, lean, False)
    places = jnp.arange(number_of)

    def named(tallies, turn):
        used = int((tallies > 0).sum())
        fixed = max(1, used // 4)
        moved = fixed + (places - fixed + turn * (used - fixed)) % max(1, number_of - fixed)
        return jnp.zeros((number_of,), jnp.int32).at[sequence[jnp.where(places < fixed, places, moved)]].set(jnp.asarray(tallies, jnp.int32))

    tallies = jnp.where(number % 4 == 0, named(packed, number // 4), named(usual, number - number // 4 - 1))
    mixed = jax.random.permutation(jax.random.fold_in(own, 3), number_of)
    source_of, taker = mixed[0:number_of // 2 * 2:2], mixed[1:number_of // 2 * 2:2]
    margin = jnp.minimum(tallies[source_of] - 1, reach - tallies[taker]) // 2
    margin = jnp.where((source_of == sequence[0]) | (taker == sequence[0]) | (tallies[taker] == 0), 0, jnp.maximum(margin, 0))
    moved = jax.random.randint(jax.random.fold_in(own, 4), (number_of // 2,), 0, 1 << 20) % (margin + 1)
    tallies = tallies.at[source_of].add(-moved).at[taker].add(moved)
    members = jnp.searchsorted(jnp.cumsum(tallies), jnp.arange(rows * top), side="right").astype(jnp.int32)
    listing = members.reshape(top, rows).T
    listing = listing[jax.random.permutation(jax.random.fold_in(own, 1), rows)]
    turn = jax.random.randint(jax.random.fold_in(own, 2), (rows, 1), 0, top)
    return jnp.take_along_axis(listing, (jnp.arange(top)[None, :] + turn) % top, axis=1)


def portions_of(amount, total, limit, lean, full):
    portions = [(1 << 20) // math.isqrt(standing ** lean) + 1 for standing in range(1, amount + 1)]
    largest = limit if full else min(limit, max(-(-total // amount), total * portions[0] // sum(portions)))
    least = 1 if total - largest >= amount - 1 else 0
    holding, surplus = [largest] + [least] * (amount - 1), total - largest - least * (amount - 1)
    while surplus > 0:
        movable = [i for i in range(1, amount) if holding[i] < largest] or [i for i in range(1, amount) if holding[i] < limit]
        whole, budget = sum([portions[i] for i in movable]), surplus
        for i in movable:
            more = min(limit - holding[i], max(1, budget * portions[i] // whole), surplus)
            holding[i] = holding[i] + more
            surplus = surplus - more
    return np.array(holding)


def gaussian(rng, shape, deviation, reach, cuts=(), held_as=jnp.bfloat16):
    values = deviation * jax.random.normal(rng, shape, jnp.float32)
    if cuts:
        values = values * levels(rng, shape, cuts, -0.22, 0.18)
    return jnp.clip(values, -reach, reach).astype(held_as)


def setup_inputs(seed: int = 0) -> dict:
    arg_keys = jax.random.split(jax.random.key(seed), 12)
    stack_input = gaussian(arg_keys[0], (MICRO, TOKENS, MODEL_WIDTH), 1.0, 6.0, ((1, 64), (2, 2)))
    output_gradient = gaussian(arg_keys[1], (MICRO, TOKENS, MODEL_WIDTH), 0.25, 1.5, ((1, 64), (2, 2)))
    norm_scale_weight = jnp.clip(1.0 + 0.1 * jax.random.normal(arg_keys[2], (LAYER_TOTAL, MODEL_WIDTH), jnp.float32), 0.5, 1.5)
    row_adapter_index_keys = jax.random.split(jax.random.fold_in(arg_keys[3], 1), MICRO * TOKENS // TOK_DEV)
    row_adapter_index_turns = jax.random.permutation(jax.random.fold_in(arg_keys[3], 3), MICRO * TOKENS // TOK_DEV)
    row_adapter_index = jax.vmap(lambda own, number: deal_out(jax.random.fold_in(arg_keys[3], 2), own, number, TOK_DEV, ADAPTER_TOTAL, 1, CAP, 2))(row_adapter_index_keys, row_adapter_index_turns).reshape((MICRO, TOKENS, 1))
    adapter_owner_index = jax.random.permutation(arg_keys[4], ADAPTER_TOTAL).astype(jnp.int32)
    adapter_down_weight = gaussian(arg_keys[5], (LAYER_TOTAL, ADAPTER_TOTAL, ADAPTER_RANK, MODEL_WIDTH), MODEL_WIDTH ** -0.5, 0.0625, ((0, 2), (1, 64)))
    adapter_up_weight = gaussian(arg_keys[6], (LAYER_TOTAL, ADAPTER_TOTAL, ADAPTER_RANK, MODEL_WIDTH), ADAPTER_RANK ** -0.5, 1.0, ((0, 2), (1, 64)))
    down_first_moment = gaussian(arg_keys[7], (LAYER_TOTAL, ADAPTER_TOTAL, ADAPTER_RANK, MODEL_WIDTH), 2.0, 12.0, ((0, 2), (1, 64)), jnp.float32)
    down_second_moment = jnp.clip(jnp.exp(math.log(1000.0) - 6.9077553 * jax.random.uniform(arg_keys[8], (LAYER_TOTAL, ADAPTER_TOTAL, ADAPTER_RANK, MODEL_WIDTH), jnp.float32) ** levels(arg_keys[8], (LAYER_TOTAL, ADAPTER_TOTAL, ADAPTER_RANK, MODEL_WIDTH), ((0, 2), (1, 64)), -0.2, 0.2)), 1.0, 1000.0)
    up_first_moment = gaussian(arg_keys[9], (LAYER_TOTAL, ADAPTER_TOTAL, ADAPTER_RANK, MODEL_WIDTH), 0.2, 1.2, ((0, 2), (1, 64)), jnp.float32)
    up_second_moment = jnp.clip(jnp.exp(math.log(10.0) - 6.9077553 * jax.random.uniform(arg_keys[10], (LAYER_TOTAL, ADAPTER_TOTAL, ADAPTER_RANK, MODEL_WIDTH), jnp.float32) ** levels(arg_keys[10], (LAYER_TOTAL, ADAPTER_TOTAL, ADAPTER_RANK, MODEL_WIDTH), ((0, 2), (1, 64)), -0.2, 0.2)), 0.01, 10.0)
    return dict(stack_input=stack_input, output_gradient=output_gradient, norm_scale_weight=norm_scale_weight, row_adapter_index=row_adapter_index, adapter_owner_index=adapter_owner_index, adapter_down_weight=adapter_down_weight, adapter_up_weight=adapter_up_weight, down_first_moment=down_first_moment, down_second_moment=down_second_moment, up_first_moment=up_first_moment, up_second_moment=up_second_moment)


adapter_scale = 0.5
beta_one = 0.9
beta_two = 0.999
step_count = 10
learn_rate = 0.001
decay_rate = 0.01
eps_root = 1e-08
eps_norm = 1e-05

def route_table(row_adapter_index, adapter_owner_index):
    labels = row_adapter_index[..., 0].reshape(MICRO, N_DP, TOK_DEV)
    matches = (labels[..., None] == jnp.arange(ADAPTER_TOTAL, dtype=jnp.int32)).astype(jnp.int32)
    target = lax.optimization_barrier(jnp.sum(matches * adapter_owner_index, axis=-1))
    alike = (target[..., :, None] == target[..., None, :]).astype(jnp.int32)
    earlier = (jnp.arange(TOK_DEV, dtype=jnp.int32)[None, :] < jnp.arange(TOK_DEV, dtype=jnp.int32)[:, None]).astype(jnp.int32)
    within = lax.optimization_barrier(jnp.sum(alike * earlier, axis=-1))
    slot_flat = target * CAP + within
    return (slot_flat[..., None, :] == jnp.arange(N_DP * CAP, dtype=jnp.int32)[:, None]).astype(jnp.float32)

def to_owners(rows, placing):
    spread = jnp.einsum('bsqt,bstd->bsqd', placing, rows.astype(jnp.float32).reshape(MICRO, N_DP, TOK_DEV, MODEL_WIDTH))
    spread = spread.reshape(MICRO, N_DP, N_DP, CAP, MODEL_WIDTH).transpose(2, 0, 1, 3, 4)
    return spread.reshape(N_DP, MICRO * N_DP * CAP, MODEL_WIDTH).astype(jnp.bfloat16)

def normalize(hidden_state, gain_row):
    value_entries = hidden_state.astype(jnp.float32)
    factor = lax.rsqrt(lax.optimization_barrier(jnp.mean(value_entries * value_entries, axis=-1, keepdims=True)) + eps_norm)
    return (value_entries, factor, (value_entries * factor * gain_row).astype(jnp.bfloat16))

def adamw_update(weight_in, moment_one, moment_two, gradient):
    first_new = beta_one * moment_one + (1.0 - beta_one) * gradient
    second_new = beta_two * moment_two + (1.0 - beta_two) * gradient * gradient
    first_hat = first_new / (1.0 - beta_one ** step_count)
    second_hat = second_new / (1.0 - beta_two ** step_count)
    value_entries = weight_in.astype(jnp.float32)
    result = value_entries - learn_rate * (first_hat / jnp.sqrt(second_hat + eps_root) + decay_rate * value_entries)
    return (result.astype(jnp.bfloat16), first_new, second_new)

def reference(stack_input, output_gradient, norm_scale_weight, row_adapter_index, adapter_owner_index, adapter_down_weight, adapter_up_weight, down_first_moment, down_second_moment, up_first_moment, up_second_moment):
    placing = route_table(row_adapter_index, adapter_owner_index)
    hidden_state = to_owners(stack_input, placing)
    arriving_input = to_owners(output_gradient, placing)
    kept = []
    for layer_position in range(LAYER_TOTAL):
        value_entries, factor, norm_output = normalize(hidden_state, norm_scale_weight[layer_position])
        rank_projection = jnp.einsum('myh,mph->myp', norm_output.astype(jnp.float32), adapter_down_weight[layer_position].astype(jnp.float32)).astype(jnp.bfloat16)
        kept.append(hidden_state)
        hidden_state = (value_entries + adapter_scale * jnp.einsum('nib,nbm->nim', rank_projection.astype(jnp.float32), adapter_up_weight[layer_position].astype(jnp.float32))).astype(jnp.bfloat16)
    grads_down = [None] * LAYER_TOTAL
    up_gradient_list = [None] * LAYER_TOTAL
    for layer_position in reversed(range(LAYER_TOTAL)):
        value_entries, factor, norm_output = normalize(kept[layer_position], norm_scale_weight[layer_position])
        rank_projection = jnp.einsum('myh,mph->myp', norm_output.astype(jnp.float32), adapter_down_weight[layer_position].astype(jnp.float32)).astype(jnp.bfloat16)
        rank_projection_gradient = (adapter_scale * jnp.einsum('myh,mph->myp', arriving_input.astype(jnp.float32), adapter_up_weight[layer_position].astype(jnp.float32))).astype(jnp.bfloat16)
        up_gradient_list[layer_position] = adapter_scale * jnp.einsum('men,meu->mnu', rank_projection.astype(jnp.float32), arriving_input.astype(jnp.float32))
        grads_down[layer_position] = jnp.einsum('men,meu->mnu', rank_projection_gradient.astype(jnp.float32), norm_output.astype(jnp.float32))
        if layer_position > 0:
            norm_output_gradient = jnp.einsum('nib,nbm->nim', rank_projection_gradient.astype(jnp.float32), adapter_down_weight[layer_position].astype(jnp.float32))
            scaled = norm_scale_weight[layer_position] * norm_output_gradient
            arriving_input = (arriving_input.astype(jnp.float32) + factor * scaled - value_entries * factor ** 3 * lax.optimization_barrier(jnp.mean(scaled * value_entries, axis=-1, keepdims=True))).astype(jnp.bfloat16)
    down_gradient = jnp.stack(grads_down)
    up_gradient = jnp.stack(up_gradient_list)
    down_weight_next, down_first_moment_next, down_second_moment_next = adamw_update(adapter_down_weight, down_first_moment, down_second_moment, down_gradient)
    up_weight_next, up_first_moment_next, up_second_moment_next = adamw_update(adapter_up_weight, up_first_moment, up_second_moment, up_gradient)
    return (down_weight_next, up_weight_next, down_first_moment_next, down_second_moment_next, up_first_moment_next, up_second_moment_next)
```

```python
import functools

import jax
import jax.numpy as jnp
from jax import lax
from jax.experimental import pallas as pl
from jax.experimental.pallas import tpu as pltpu
from jax.sharding import PartitionSpec as P

adapter_scale = 0.5
beta_one = 0.9
beta_two = 0.999
step_count = 10
learn_rate = 0.001
decay_rate = 0.01
eps_root = 1e-08
eps_norm = 1e-05

MESH = pl.DeviceIdType.MESH
F32 = jnp.float32
BF16 = jnp.bfloat16
RANK = 32
WIDTH = 8192
HALF = 4096
OWNERS = 64
CAP = 4
ROWS = 128
PIECE = 16
GROUPS = 8
MEMBERS = OWNERS // GROUPS
GROUP_ROWS = MEMBERS * PIECE
SPLIT = 4
PART = HALF // SPLIT
AHEAD = 3
STRIDE = 27
TILE = 1024


def partner_of(position):
    dp = lax.axis_index("dp")
    core, x_hi, y, z = dp % 2, (dp // 2) % 2, (dp // 4) % 4, dp // 16
    offset = (STRIDE * position) % OWNERS
    dz, dy, dx, dc = offset // 16, (offset // 4) % 4, (offset // 2) % 2, offset % 2
    dz = (dz + core * (4 - 2 * dz)) % 4
    dy = (dy + core * (4 - 2 * dy)) % 4
    return (((z + dz) % 4 * 4 + (y + dy) % 4) * 2 + (x_hi + dx) % 2) * 2 + (core + dc) % 2


def place_rows(labels_ref, owner_ref):
    lane = lax.broadcasted_iota(jnp.int32, (ROWS, ROWS), 1)
    line = lax.broadcasted_iota(jnp.int32, (ROWS, ROWS), 0)
    owner_row = owner_ref[...].astype(F32)
    parts = []
    for micro in range(2):
        label = jnp.broadcast_to(labels_ref[micro], (ROWS, ROWS)).astype(F32)
        label_row = label.T
        within = jnp.sum(
            jnp.where((label == label_row) & (lane < line), 1.0, 0.0), axis=1, keepdims=True
        )
        target = jnp.sum(
            jnp.where(label[:, :OWNERS] == lane[:, :OWNERS].astype(F32), owner_row, 0.0),
            axis=1,
            keepdims=True,
        )
        slot = jnp.broadcast_to(target * (2 * CAP) + micro * CAP + within, (ROWS, ROWS)).T[:1, :]
        want = lax.broadcasted_iota(jnp.int32, (OWNERS * 2 * CAP, ROWS), 0).astype(F32)
        parts.append(jnp.where(want == slot, 1.0, 0.0))
    return jnp.concatenate(parts, axis=1).astype(BF16)


def row_factors(total_h, total_g, gram):
    dot = functools.partial(jnp.dot, preferred_element_type=F32, precision=lax.Precision.HIGHEST)
    squares = total_h[:, 96:97]
    r0 = lax.rsqrt(squares * (1.0 / WIDTH) + eps_norm)
    low0 = (r0 * total_h[:, 0:32]).astype(BF16).astype(F32)
    moved = dot(low0, gram[32:64, :])
    h1_up0 = total_h[:, 32:64] + adapter_scale * moved[:, 32:64]
    h1_down1 = total_h[:, 64:96] + adapter_scale * moved[:, 64:96]
    squares1 = squares + jnp.sum(
        low0 * (2 * adapter_scale * total_h[:, 32:64] + adapter_scale**2 * moved[:, 32:64]),
        axis=1,
        keepdims=True,
    )
    r1 = lax.rsqrt(jnp.maximum(squares1, 0.0) * (1.0 / WIDTH) + eps_norm)
    low1 = (r1 * h1_down1).astype(BF16).astype(F32)
    lg1 = (adapter_scale * total_g[:, 96:128]).astype(BF16).astype(F32)
    mean = jnp.sum(lg1 * h1_down1, axis=1, keepdims=True) * (1.0 / WIDTH)
    cube = r1 * r1 * r1 * mean
    scaled1 = r1 * lg1
    g1_up0 = total_g[:, 32:64] + dot(scaled1, gram[64:96, :])[:, 32:64] - cube * h1_up0
    lg0 = (adapter_scale * g1_up0).astype(BF16).astype(F32)
    zero = jnp.zeros_like(low0)
    for_h = jnp.concatenate([r0 * lg0, -cube * low0, scaled1, zero], axis=1)
    for_g = jnp.concatenate([zero, low0, zero, low1], axis=1)
    cross_h = jnp.concatenate([zero, low0, zero, zero], axis=1)
    cross_g = jnp.concatenate([zero, zero, scaled1, zero], axis=1)
    return for_h, for_g, cross_h, cross_g


def interleave(upper, lower):
    columns = upper.shape[-1]
    both = jnp.concatenate(
        [upper.reshape(-1, 8, columns), lower.reshape(-1, 8, columns)], axis=1
    )
    return both.astype(BF16)


def gradient_kernel(
    h_hbm,
    g_hbm,
    gain_ref,
    labels_ref,
    owner_ref,
    down_ref,
    up_ref,
    grad_ref,
    h_in,
    g_in,
    send,
    recv,
    weights,
    weights_out,
    products,
    products_in,
    gram,
    total,
    cross,
    grad_out,
    in_sem,
    send_sem,
    recv_sem,
    weight_sem,
    product_send_sem,
    product_sem,
    grad_sem,
):
    pipe = lax.axis_index("pipe")
    dp = lax.axis_index("dp")
    other = (1 - pipe, dp)

    copy_h = pltpu.make_async_copy(h_hbm, h_in, in_sem.at[0])
    copy_g = pltpu.make_async_copy(g_hbm, g_in, in_sem.at[1])
    copy_h.start()
    copy_g.start()

    barrier = pltpu.get_barrier_semaphore()

    @pl.loop(1, OWNERS)
    def _(i):
        pl.semaphore_signal(barrier, inc=1, device_id=(pipe, partner_of(i)), device_id_type=MESH)

    pl.semaphore_signal(barrier, inc=1, device_id=other, device_id_type=MESH)

    mine = pl.ds(pl.multiple_of(pipe * HALF, HALF), HALF)
    theirs = pl.ds(pl.multiple_of((1 - pipe) * HALF, HALF), HALF)
    layer = pl.ds(pl.multiple_of(pipe * 2 * RANK, 2 * RANK), 2 * RANK)
    weights_out[0:RANK, :] = (down_ref[:, theirs].astype(F32) * gain_ref[:, theirs]).astype(BF16)
    weights_out[RANK:, :] = up_ref[:, theirs]
    weights[pl.ds(pl.multiple_of(pipe * 2 * RANK, 2 * RANK), RANK), :] = (
        down_ref[:, mine].astype(F32) * gain_ref[:, mine]
    ).astype(BF16)
    weights[pl.ds(pl.multiple_of(pipe * 2 * RANK + RANK, RANK), RANK), :] = up_ref[:, mine]
    placing = place_rows(labels_ref, owner_ref)
    total[...] = jnp.zeros_like(total)
    cross[...] = jnp.zeros_like(cross)

    copy_h.wait()
    copy_g.wait()
    pl.semaphore_wait(barrier, OWNERS)
    copy_weights = pltpu.make_async_remote_copy(
        src_ref=weights_out,
        dst_ref=weights.at[layer],
        send_sem=weight_sem.at[0],
        recv_sem=weight_sem.at[1],
        device_id=other,
        device_id_type=MESH,
    )
    copy_weights.start()

    def start_part(place, part):
        target = partner_of(place)
        columns = pl.ds(pl.multiple_of(part * PART, PART), PART)
        pltpu.make_async_remote_copy(
            src_ref=send.at[target, :, columns],
            dst_ref=recv.at[place, :, columns],
            send_sem=send_sem,
            recv_sem=recv_sem.at[place // MEMBERS],
            device_id=(pipe, target),
            device_id_type=MESH,
        ).start()

    for part in range(SPLIT):
        columns = slice(part * PART, (part + 1) * PART)
        packed_h = jnp.dot(
            placing, h_in[:, :, columns].reshape(2 * ROWS, PART), preferred_element_type=F32
        )
        packed_g = jnp.dot(
            placing, g_in[:, :, columns].reshape(2 * ROWS, PART), preferred_element_type=F32
        )
        send[:, :, columns] = interleave(packed_h, packed_g)

        @pl.loop(1, AHEAD * MEMBERS)
        def _(i):
            start_part(i, part)

    copy_self = pltpu.make_async_copy(send.at[dp], recv.at[0], recv_sem.at[0])
    copy_self.start()

    def start_products(slot):
        pltpu.make_async_remote_copy(
            src_ref=products.at[slot],
            dst_ref=products_in.at[slot],
            send_sem=product_send_sem,
            recv_sem=product_sem.at[slot],
            device_id=other,
            device_id_type=MESH,
        ).start()

    def wait_products(slot):
        pltpu.make_async_copy(
            products_in.at[slot], products_in.at[slot], product_sem.at[slot]
        ).wait()

    copy_weights.wait()
    products[GROUPS] = lax.dot_general(
        weights[...], weights[...], (((1,), (1,)), ((), ())), preferred_element_type=F32
    )
    start_products(GROUPS)
    wait_products(GROUPS)
    gram[...] = products[GROUPS] + products_in[GROUPS]

    @pl.loop(0, GROUPS + 1)
    def _(group):
        @pl.when(group < GROUPS)
        def _():
            members = pl.ds(group * MEMBERS, MEMBERS)
            pltpu.make_async_copy(recv.at[members], recv.at[members], recv_sem.at[group]).wait()

            @pl.when(group + AHEAD < GROUPS)
            def _():
                @pl.loop(0, SPLIT)
                def _(part):
                    @pl.loop(0, MEMBERS)
                    def _(i):
                        start_part((group + AHEAD) * MEMBERS + i, part)

            product = jnp.zeros((GROUP_ROWS, 4 * RANK), F32)
            squares = jnp.zeros((GROUP_ROWS, ROWS), F32)
            for tile in range(HALF // TILE):
                columns = slice(tile * TILE, (tile + 1) * TILE)
                rows = recv[members, :, columns].reshape(GROUP_ROWS, TILE)
                product += lax.dot_general(
                    rows,
                    weights[:, columns],
                    (((1,), (1,)), ((), ())),
                    preferred_element_type=F32,
                )
                wide = rows.astype(F32)
                for k in range(TILE // ROWS):
                    piece = wide[:, k * ROWS : (k + 1) * ROWS]
                    squares += piece * piece
            line = lax.broadcasted_iota(jnp.int32, product.shape, 0) % PIECE
            lane = lax.broadcasted_iota(jnp.int32, product.shape, 1)
            products[group] = jnp.where(
                (line < 8) & (lane >= 3 * RANK), jnp.sum(squares, axis=1, keepdims=True), product
            )
            start_products(group)

        @pl.when(group > 0)
        def _():
            done = group - 1
            wait_products(done)
            both = (products[done] + products_in[done]).reshape(MEMBERS, PIECE, 4 * RANK)
            for_h, for_g, cross_h, cross_g = row_factors(
                both[:, :8, :].reshape(-1, 4 * RANK), both[:, 8:, :].reshape(-1, 4 * RANK), gram[...]
            )
            factors = interleave(for_h, for_g).reshape(GROUP_ROWS, 4 * RANK)
            beside = interleave(cross_h, cross_g).reshape(GROUP_ROWS, 4 * RANK)
            over_rows = (((0,), (0,)), ((), ()))
            cross[...] += lax.dot_general(factors, beside, over_rows, preferred_element_type=F32)
            members = pl.ds(done * MEMBERS, MEMBERS)
            for tile in range(HALF // TILE):
                columns = slice(tile * TILE, (tile + 1) * TILE)
                rows = recv[members, :, columns].reshape(GROUP_ROWS, TILE)
                total[:, columns] += lax.dot_general(
                    factors, rows, over_rows, preferred_element_type=F32
                )

    line = lax.broadcasted_iota(jnp.int32, cross.shape, 0) // RANK
    lane = lax.broadcasted_iota(jnp.int32, cross.shape, 1) // RANK
    keep = jnp.where((lane == 1) & ((line == 1) | (line == 2)), adapter_scale, 0.0)
    keep = jnp.where((lane == 2) & (line == 1), 1.0, keep)
    cross[...] = cross[...] * keep
    row = lax.broadcasted_iota(jnp.int32, (2 * RANK, TILE), 0)
    scale = jnp.where(row < RANK, 1.0, adapter_scale)

    def finish(tile, section):
        columns = slice(tile * TILE, (tile + 1) * TILE)
        at = pl.ds(pl.multiple_of(section * 2 * RANK, 2 * RANK), 2 * RANK)
        whole = total[at, columns] + jnp.dot(
            cross[at, :].astype(BF16), weights[:, columns], preferred_element_type=F32
        )
        return (whole * scale).astype(BF16)

    sent = []
    for side, section in enumerate((1 - pipe, pipe)):
        for tile in range(HALF // TILE):
            columns = slice(tile * TILE, (tile + 1) * TILE)
            grad_out[side, :, columns] = finish(tile, section)
            placed = grad_ref.at[:, pl.ds(pl.multiple_of(pipe * HALF + tile * TILE, TILE), TILE)]
            if side == 0:
                copy = pltpu.make_async_remote_copy(
                    src_ref=grad_out.at[0, :, columns],
                    dst_ref=placed,
                    send_sem=grad_sem.at[0, tile],
                    recv_sem=grad_sem.at[1, tile],
                    device_id=other,
                    device_id_type=MESH,
                )
            else:
                copy = pltpu.make_async_copy(
                    grad_out.at[1, :, columns], placed, grad_sem.at[2, tile]
                )
            copy.start()
            sent.append(copy)
    pltpu.make_async_copy(send.at[pl.ds(1, 63)], send.at[pl.ds(1, 63)], send_sem).wait()
    pltpu.make_async_copy(products, products, product_send_sem).wait()
    for copy in sent:
        copy.wait()


def gradients(stack_input, output_gradient, gain, labels, owners, down, up):
    anywhere = pl.BlockSpec(memory_space=pl.ANY)
    whole = pl.BlockSpec(memory_space=pltpu.VMEM)
    return pl.pallas_call(
        gradient_kernel,
        out_shape=jax.ShapeDtypeStruct((2 * RANK, WIDTH), BF16),
        in_specs=[anywhere, anywhere, whole, whole, whole, whole, whole],
        out_specs=anywhere,
        scratch_shapes=[
            pltpu.VMEM((2, ROWS, HALF), BF16),
            pltpu.VMEM((2, ROWS, HALF), BF16),
            pltpu.VMEM((OWNERS, PIECE, HALF), BF16),
            pltpu.VMEM((OWNERS, PIECE, HALF), BF16),
            pltpu.VMEM((4 * RANK, HALF), BF16),
            pltpu.VMEM((2 * RANK, HALF), BF16),
            pltpu.VMEM((GROUPS + 1, GROUP_ROWS, 4 * RANK), F32),
            pltpu.VMEM((GROUPS + 1, GROUP_ROWS, 4 * RANK), F32),
            pltpu.VMEM((4 * RANK, 4 * RANK), F32),
            pltpu.VMEM((4 * RANK, HALF), F32),
            pltpu.VMEM((4 * RANK, 4 * RANK), F32),
            pltpu.VMEM((2, 2 * RANK, HALF), BF16),
            pltpu.SemaphoreType.DMA((2,)),
            pltpu.SemaphoreType.DMA(()),
            pltpu.SemaphoreType.DMA((GROUPS,)),
            pltpu.SemaphoreType.DMA((2,)),
            pltpu.SemaphoreType.DMA(()),
            pltpu.SemaphoreType.DMA((GROUPS + 1,)),
            pltpu.SemaphoreType.DMA((3, HALF // TILE)),
        ],
        compiler_params=pltpu.CompilerParams(
            collective_id=0, has_side_effects=True, vmem_limit_bytes=56 * 2**20
        ),
    )(stack_input, output_gradient, gain, labels, owners, down, up)


def adamw_kernel(
    grad_ref,
    gain_ref,
    down_ref,
    up_ref,
    down_m_ref,
    down_v_ref,
    up_m_ref,
    up_v_ref,
    down_out,
    up_out,
    down_m_out,
    down_v_out,
    up_m_out,
    up_v_out,
):
    def update(weight, one, two, gradient, weight_out, one_out, two_out):
        first_new = beta_one * one[...] + (1.0 - beta_one) * gradient
        second_new = beta_two * two[...] + (1.0 - beta_two) * gradient * gradient
        first_hat = first_new / (1.0 - beta_one**step_count)
        second_hat = second_new / (1.0 - beta_two**step_count)
        value = weight[...].astype(F32)
        result = value - learn_rate * (
            first_hat / jnp.sqrt(second_hat + eps_root) + decay_rate * value
        )
        weight_out[...] = result.astype(BF16)
        one_out[...] = first_new
        two_out[...] = second_new

    down_gradient = grad_ref[0:RANK, :].astype(F32) * gain_ref[...]
    update(down_ref, down_m_ref, down_v_ref, down_gradient, down_out, down_m_out, down_v_out)
    update(up_ref, up_m_ref, up_v_ref, grad_ref[RANK:, :].astype(F32), up_out, up_m_out, up_v_out)


def adamw(grad, gain, down, up, down_m, down_v, up_m, up_v):
    tile = 1024
    across = pl.BlockSpec((RANK, tile), lambda j: (0, j))
    shape = lambda dtype: jax.ShapeDtypeStruct((RANK, WIDTH), dtype)
    return pl.pallas_call(
        adamw_kernel,
        grid=(WIDTH // tile,),
        in_specs=[
            pl.BlockSpec((2 * RANK, tile), lambda j: (0, j)),
            pl.BlockSpec((1, tile), lambda j: (0, j)),
        ]
        + [across] * 6,
        out_specs=[across] * 6,
        out_shape=[shape(BF16), shape(BF16), shape(F32), shape(F32), shape(F32), shape(F32)],
    )(grad, gain, down, up, down_m, down_v, up_m, up_v)


def body(
    stack_input,
    output_gradient,
    norm_scale_weight,
    row_adapter_index,
    adapter_owner_index,
    adapter_down_weight,
    adapter_up_weight,
    down_first_moment,
    down_second_moment,
    up_first_moment,
    up_second_moment,
):
    down, up, down_m, down_v, up_m, up_v = (
        array.reshape(RANK, WIDTH)
        for array in (
            adapter_down_weight,
            adapter_up_weight,
            down_first_moment,
            down_second_moment,
            up_first_moment,
            up_second_moment,
        )
    )
    grad = gradients(
        stack_input,
        output_gradient,
        norm_scale_weight,
        row_adapter_index,
        adapter_owner_index.reshape(1, OWNERS),
        down,
        up,
    )
    results = adamw(grad, norm_scale_weight, down, up, down_m, down_v, up_m, up_v)
    return tuple(array.reshape(1, 1, RANK, WIDTH) for array in results)


def solution(mesh):
    by_owner = P("pipe", "dp", None, None)
    return jax.shard_map(
        body,
        mesh=mesh,
        in_specs=(
            P(None, "dp", "pipe"),
            P(None, "dp", "pipe"),
            P("pipe", None),
            P(None, "dp", None),
            P(),
        )
        + (by_owner,) * 6,
        out_specs=(by_owner,) * 6,
        check_vma=False,
    )
```

```python
import functools

import jax
import jax.numpy as jnp
from jax import lax
from jax.experimental import pallas as pl
from jax.experimental.pallas import tpu as pltpu
from jax.sharding import PartitionSpec as P

adapter_scale = 0.5
beta_one = 0.9
beta_two = 0.999
step_count = 10
learn_rate = 0.001
decay_rate = 0.01
eps_root = 1e-08
eps_norm = 1e-05

MESH = pl.DeviceIdType.MESH
F32 = jnp.float32
BF16 = jnp.bfloat16
RANK = 32
WIDTH = 8192
HALF = 4096
OWNERS = 64
CAP = 4
ROWS = 128
PIECE = 16
GROUPS = 8
MEMBERS = OWNERS // GROUPS
HALF_ROWS = MEMBERS // 2 * PIECE
CROSSED = 8
GROUP_ROWS = MEMBERS * PIECE
SPLIT = 4
PART = HALF // SPLIT
AHEAD = 3
DEFER = 1
TILE = 1024
UPDATE_TILE = 1024


def partner_of(place):
    pipe, dp = lax.axis_index("pipe"), lax.axis_index("dp")
    core, x_hi, y, z = dp % 2, (dp // 2) % 2, (dp // 4) % 4, dp // 16
    group, member = place // MEMBERS, place % MEMBERS
    dx = member // (MEMBERS // 2)
    rank = group * (MEMBERS // 2) + member % (MEMBERS // 2)
    odd = (rank // 16 + dx) % 2
    mixed = (5 * (rank % 16)) % 16
    dz, dc = mixed // 4, mixed % 2
    dy = 2 * ((mixed // 2) % 2) + (odd + dz) % 2
    dz = (dz + core * (4 - 2 * dz)) % 4
    dy = (dy + core * (4 - 2 * dy)) % 4
    target = (((z + dz) % 4 * 4 + (y + dy) % 4) * 2 + (x_hi + dx) % 2) * 2 + (core + dc) % 2
    return (pipe + dx * crossed(group)) % 2, target


def crossed(group):
    return (GROUPS - 1 - group + CROSSED) // GROUPS


def place_rows(labels_ref, owner_ref):
    lane = lax.broadcasted_iota(jnp.int32, (ROWS, ROWS), 1)
    line = lax.broadcasted_iota(jnp.int32, (ROWS, ROWS), 0)
    owner_row = owner_ref[...].astype(F32)
    parts = []
    for micro in range(2):
        label_row = jnp.broadcast_to(labels_ref[micro : micro + 1, :].astype(F32), (ROWS, ROWS))
        label = label_row.T
        within = jnp.sum(
            jnp.where((label == label_row) & (lane < line), 1.0, 0.0), axis=1, keepdims=True
        )
        target = jnp.sum(
            jnp.where(label[:, :OWNERS] == lane[:, :OWNERS].astype(F32), owner_row, 0.0),
            axis=1,
            keepdims=True,
        )
        slot = jnp.broadcast_to(target * (2 * CAP) + micro * CAP + within, (ROWS, ROWS)).T[:1, :]
        want = lax.broadcasted_iota(jnp.int32, (OWNERS * 2 * CAP, ROWS), 0).astype(F32)
        parts.append(jnp.where(want == slot, 1.0, 0.0))
    return jnp.concatenate(parts, axis=1).astype(BF16)


def row_factors(total_h, total_g, gram):
    dot = functools.partial(jnp.dot, preferred_element_type=F32, precision=lax.Precision.HIGHEST)
    squares = total_h[:, 96:97]
    r0 = lax.rsqrt(squares * (1.0 / WIDTH) + eps_norm)
    low0 = (r0 * total_h[:, 0:32]).astype(BF16).astype(F32)
    moved = dot(low0, gram[32:64, :])
    h1_up0 = total_h[:, 32:64] + adapter_scale * moved[:, 32:64]
    h1_down1 = total_h[:, 64:96] + adapter_scale * moved[:, 64:96]
    squares1 = squares + jnp.sum(
        low0 * (2 * adapter_scale * total_h[:, 32:64] + adapter_scale**2 * moved[:, 32:64]),
        axis=1,
        keepdims=True,
    )
    r1 = lax.rsqrt(jnp.maximum(squares1, 0.0) * (1.0 / WIDTH) + eps_norm)
    low1 = (r1 * h1_down1).astype(BF16).astype(F32)
    lg1 = (adapter_scale * total_g[:, 96:128]).astype(BF16).astype(F32)
    mean = jnp.sum(lg1 * h1_down1, axis=1, keepdims=True) * (1.0 / WIDTH)
    cube = r1 * r1 * r1 * mean
    scaled1 = r1 * lg1
    g1_up0 = total_g[:, 32:64] + dot(scaled1, gram[64:96, :])[:, 32:64] - cube * h1_up0
    lg0 = (adapter_scale * g1_up0).astype(BF16).astype(F32)
    zero = jnp.zeros_like(low0)
    for_h = jnp.concatenate([r0 * lg0, -cube * low0, scaled1, zero], axis=1)
    for_g = jnp.concatenate([zero, low0, zero, low1], axis=1)
    cross_h = jnp.concatenate([zero, low0, zero, zero], axis=1)
    cross_g = jnp.concatenate([zero, zero, scaled1, zero], axis=1)
    return for_h, for_g, cross_h, cross_g


def interleave(upper, lower):
    columns = upper.shape[-1]
    both = jnp.concatenate(
        [upper.reshape(-1, 8, columns), lower.reshape(-1, 8, columns)], axis=1
    )
    return both.astype(BF16)


def gradient_kernel(
    h_hbm,
    g_hbm,
    gain_hbm,
    labels_hbm,
    owner_hbm,
    down_hbm,
    up_hbm,
    grad_ref,
    h_in,
    g_in,
    gain_ref,
    labels_ref,
    owner_ref,
    down_ref,
    up_ref,
    send,
    recv,
    weights,
    products,
    products_in,
    gram,
    total,
    cross,
    grad_out,
    grad_in,
    in_sem,
    send_sem,
    recv_sem,
    weight_sem,
    product_send_sem,
    product_sem,
    grad_sem,
):
    pipe = lax.axis_index("pipe")
    dp = lax.axis_index("dp")
    other = (1 - pipe, dp)

    copies_in = [
        pltpu.make_async_copy(*pair, in_sem.at[n])
        for n, pair in enumerate(
            (
                (labels_hbm, labels_ref),
                (owner_hbm, owner_ref),
                (h_hbm, h_in),
                (g_hbm, g_in),
                (gain_hbm, gain_ref),
                (down_hbm, down_ref),
                (up_hbm, up_ref),
            )
        )
    ]
    for copy in copies_in:
        copy.start()

    barrier = pltpu.get_barrier_semaphore()

    @pl.loop(1, OWNERS)
    def _(i):
        pl.semaphore_signal(barrier, inc=1, device_id=partner_of(i), device_id_type=MESH)

    pl.semaphore_signal(barrier, inc=1, device_id=other, device_id_type=MESH)

    layer = pl.ds(pl.multiple_of(pipe * 2 * RANK, 2 * RANK), 2 * RANK)
    copies_in[0].wait()
    copies_in[1].wait()
    placing = place_rows(labels_ref, owner_ref)
    copies_in[2].wait()
    copies_in[3].wait()

    pl.semaphore_wait(barrier, OWNERS)

    def weight_copy(side, part):
        columns = slice(part * PART, (part + 1) * PART)
        return pltpu.make_async_remote_copy(
            src_ref=weights.at[1 - side, layer, columns],
            dst_ref=weights.at[side, layer, columns],
            send_sem=weight_sem.at[0, side, part],
            recv_sem=weight_sem.at[1, side, part],
            device_id=other,
            device_id_type=MESH,
        )

    def start_part(place, part):
        target = partner_of(place)
        columns = pl.ds(pl.multiple_of(part * PART, PART), PART)
        pltpu.make_async_remote_copy(
            src_ref=send.at[target[1], :, columns],
            dst_ref=recv.at[place, :, columns],
            send_sem=send_sem,
            recv_sem=recv_sem.at[place // MEMBERS],
            device_id=target,
            device_id_type=MESH,
        ).start()

    def start_group(group, part, first=0):
        @pl.loop(first, MEMBERS)
        def _(i):
            start_part(group * MEMBERS + i % 2 * (MEMBERS // 2) + i // 2, part)

    def prepare_weights():
        for copy in copies_in[4:]:
            copy.wait()
        for side, half in enumerate((pipe, 1 - pipe)):
            columns = pl.ds(pl.multiple_of(half * HALF, HALF), HALF)
            weights[side, pl.ds(pl.multiple_of(pipe * 2 * RANK, RANK), RANK), :] = (
                down_ref[:, columns].astype(F32) * gain_ref[:, columns]
            ).astype(BF16)
            weights[side, pl.ds(pl.multiple_of(pipe * 2 * RANK + RANK, RANK), RANK), :] = up_ref[
                :, columns
            ]

    for part in range(SPLIT):
        columns = slice(part * PART, (part + 1) * PART)
        packed_h = jnp.dot(
            placing, h_in[:, :, columns].reshape(2 * ROWS, PART), preferred_element_type=F32
        )
        packed_g = jnp.dot(
            placing, g_in[:, :, columns].reshape(2 * ROWS, PART), preferred_element_type=F32
        )
        send[:, :, columns] = interleave(packed_h, packed_g)
        start_group(0, part, 1)
        if part == 0:
            prepare_weights()
        weight_copy(0, part).start()
        weight_copy(1, part).start()

    @pl.loop(1, AHEAD)
    def _(group):
        @pl.loop(0, SPLIT)
        def _(part):
            start_group(group, part)

    copy_self = pltpu.make_async_copy(send.at[dp], recv.at[0], recv_sem.at[0])
    copy_self.start()
    total[...] = jnp.zeros_like(total)
    cross[...] = jnp.zeros_like(cross)

    def start_products(slot):
        pltpu.make_async_remote_copy(
            src_ref=products.at[slot],
            dst_ref=products_in.at[slot],
            send_sem=product_send_sem,
            recv_sem=product_sem.at[slot],
            device_id=other,
            device_id_type=MESH,
        ).start()

    def wait_products(slot):
        pltpu.make_async_copy(
            products_in.at[slot], products_in.at[slot], product_sem.at[slot]
        ).wait()

    for side in range(2):
        for part in range(SPLIT):
            weight_copy(side, part).wait()
    products[GROUPS] = lax.dot_general(
        weights[0], weights[0], (((1,), (1,)), ((), ())), preferred_element_type=F32
    )
    start_products(GROUPS)

    row = lax.broadcasted_iota(jnp.int32, (2 * RANK, TILE), 0)
    scale = jnp.where(row < RANK, 1.0, adapter_scale)

    def mask_cross(side):
        line = lax.broadcasted_iota(jnp.int32, (4 * RANK, 4 * RANK), 0) // RANK
        lane = lax.broadcasted_iota(jnp.int32, (4 * RANK, 4 * RANK), 1) // RANK
        keep = jnp.where((lane == 1) & ((line == 1) | (line == 2)), adapter_scale, 0.0)
        keep = jnp.where((lane == 2) & (line == 1), 1.0, keep)
        cross[side] = cross[side] * keep

    def finish(side, section, columns):
        at = pl.ds(pl.multiple_of(section * 2 * RANK, 2 * RANK), 2 * RANK)
        whole = total[side, at, columns] + jnp.dot(
            cross[side, at, :].astype(BF16),
            weights[side, :, columns],
            preferred_element_type=F32,
        )
        return whole * scale

    def grad_copy(side, tile):
        columns = slice(tile * TILE, (tile + 1) * TILE)
        return pltpu.make_async_remote_copy(
            src_ref=grad_out.at[side, :, columns],
            dst_ref=grad_in.at[side, :, columns],
            send_sem=grad_sem.at[0, side, tile],
            recv_sem=grad_sem.at[1, side, tile],
            device_id=other,
            device_id_type=MESH,
        )

    def hand_over(side):
        mask_cross(side)
        for tile in range(HALF // TILE):
            columns = slice(tile * TILE, (tile + 1) * TILE)
            grad_out[side, :, columns] = finish(side, 1 - pipe, columns).astype(BF16)
            grad_copy(side, tile).start()

    by_rows = (((1,), (1,)), ((), ()))
    over_rows = (((0,), (0,)), ((), ()))

    @pl.loop(0, GROUPS + DEFER)
    def _(group):
        @pl.when(group < GROUPS)
        def _():
            first = group * MEMBERS
            members = pl.ds(first, MEMBERS)
            pltpu.make_async_copy(recv.at[members], recv.at[members], recv_sem.at[group]).wait()
            halves = [
                (pl.ds(first, MEMBERS // 2), 0),
                (pl.ds(first + MEMBERS // 2, MEMBERS // 2), crossed(group)),
            ]
            product = [jnp.zeros((HALF_ROWS, 4 * RANK), F32) for _ in halves]
            squares = [jnp.zeros((HALF_ROWS, ROWS), F32) for _ in halves]
            for tile in range(HALF // TILE):
                columns = slice(tile * TILE, (tile + 1) * TILE)
                for n, (half, side) in enumerate(halves):
                    rows = recv[half, :, columns].reshape(HALF_ROWS, TILE)
                    product[n] += lax.dot_general(
                        rows, weights[side, :, columns], by_rows, preferred_element_type=F32
                    )
                    wide = rows.astype(F32)
                    for k in range(TILE // ROWS):
                        piece = wide[:, k * ROWS : (k + 1) * ROWS]
                        squares[n] += piece * piece
            product = jnp.concatenate(product, axis=0)
            squares = jnp.sum(jnp.concatenate(squares, axis=0), axis=1, keepdims=True)
            line = lax.broadcasted_iota(jnp.int32, product.shape, 0) % PIECE
            lane = lax.broadcasted_iota(jnp.int32, product.shape, 1)
            products[group] = jnp.where((line < 8) & (lane >= 3 * RANK), squares, product)
            start_products(group)

            @pl.when(group + AHEAD < GROUPS)
            def _():
                @pl.loop(0, SPLIT)
                def _(part):
                    start_group(group + AHEAD, part)

        @pl.when(group == DEFER)
        def _():
            wait_products(GROUPS)
            gram[...] = products[GROUPS] + products_in[GROUPS]

        @pl.when(group >= DEFER)
        def _():
            done = group - DEFER
            wait_products(done)
            both = (products[done] + products_in[done]).reshape(MEMBERS, PIECE, 4 * RANK)
            for_h, for_g, cross_h, cross_g = row_factors(
                both[:, :8, :].reshape(-1, 4 * RANK), both[:, 8:, :].reshape(-1, 4 * RANK), gram[...]
            )
            factors = interleave(for_h, for_g).reshape(GROUP_ROWS, 4 * RANK)
            beside = interleave(cross_h, cross_g).reshape(GROUP_ROWS, 4 * RANK)
            first = done * MEMBERS

            def add(rows_at, picked, side):
                cross[side] += lax.dot_general(
                    factors[picked], beside[picked], over_rows, preferred_element_type=F32
                )
                for tile in range(HALF // TILE):
                    columns = slice(tile * TILE, (tile + 1) * TILE)
                    rows = recv[rows_at, :, columns].reshape(-1, TILE)
                    total[side, :, columns] += lax.dot_general(
                        factors[picked], rows, over_rows, preferred_element_type=F32
                    )

            @pl.when(done < CROSSED)
            def _():
                add(pl.ds(first, MEMBERS // 2), slice(0, HALF_ROWS), 0)
                add(pl.ds(first + MEMBERS // 2, MEMBERS // 2), slice(HALF_ROWS, None), 1)

            @pl.when(done >= CROSSED)
            def _():
                add(pl.ds(first, MEMBERS), slice(None), 0)

            @pl.when(done == CROSSED - 1)
            def _():
                hand_over(1)

    hand_over(0)
    for side, half in enumerate((pipe, 1 - pipe)):
        for tile in range(HALF // TILE):
            columns = slice(tile * TILE, (tile + 1) * TILE)
            mine = finish(side, pipe, columns)
            grad_copy(1 - side, tile).wait()
            at = pl.ds(pl.multiple_of(half * HALF + tile * TILE, TILE), TILE)
            grad_ref[:, at] = mine + grad_in[1 - side, :, columns].astype(F32)
    pltpu.make_async_copy(send.at[pl.ds(1, 63)], send.at[pl.ds(1, 63)], send_sem).wait()
    pltpu.make_async_copy(products, products, product_send_sem).wait()


def gradients(stack_input, output_gradient, gain, labels, owners, down, up):
    whole = pl.BlockSpec(memory_space=pltpu.VMEM)
    return pl.pallas_call(
        gradient_kernel,
        out_shape=jax.ShapeDtypeStruct((2 * RANK, WIDTH), F32),
        in_specs=[pl.BlockSpec(memory_space=pl.ANY)] * 7,
        out_specs=whole,
        scratch_shapes=[
            pltpu.VMEM((2, ROWS, HALF), BF16),
            pltpu.VMEM((2, ROWS, HALF), BF16),
            pltpu.VMEM((1, WIDTH), F32),
            pltpu.VMEM((2, ROWS), jnp.int32),
            pltpu.VMEM((1, OWNERS), jnp.int32),
            pltpu.VMEM((RANK, WIDTH), BF16),
            pltpu.VMEM((RANK, WIDTH), BF16),
            pltpu.VMEM((OWNERS, PIECE, HALF), BF16),
            pltpu.VMEM((OWNERS, PIECE, HALF), BF16),
            pltpu.VMEM((2, 4 * RANK, HALF), BF16),
            pltpu.VMEM((GROUPS + 1, GROUP_ROWS, 4 * RANK), F32),
            pltpu.VMEM((GROUPS + 1, GROUP_ROWS, 4 * RANK), F32),
            pltpu.VMEM((4 * RANK, 4 * RANK), F32),
            pltpu.VMEM((2, 4 * RANK, HALF), F32),
            pltpu.VMEM((2, 4 * RANK, 4 * RANK), F32),
            pltpu.VMEM((2, 2 * RANK, HALF), BF16),
            pltpu.VMEM((2, 2 * RANK, HALF), BF16),
            pltpu.SemaphoreType.DMA((7,)),
            pltpu.SemaphoreType.DMA(()),
            pltpu.SemaphoreType.DMA((GROUPS,)),
            pltpu.SemaphoreType.DMA((2, 2, SPLIT)),
            pltpu.SemaphoreType.DMA(()),
            pltpu.SemaphoreType.DMA((GROUPS + 1,)),
            pltpu.SemaphoreType.DMA((2, 2, HALF // TILE)),
        ],
        compiler_params=pltpu.CompilerParams(
            collective_id=0, has_side_effects=True, vmem_limit_bytes=56 * 2**20
        ),
    )(stack_input, output_gradient, gain, labels, owners, down, up)


def adamw_kernel(
    grad_ref,
    gain_ref,
    down_ref,
    up_ref,
    down_m_ref,
    down_v_ref,
    up_m_ref,
    up_v_ref,
    down_out,
    up_out,
    down_m_out,
    down_v_out,
    up_m_out,
    up_v_out,
    weights_new,
    moments_new,
    sem,
):
    outs = ((down_out, down_m_out, down_v_out), (up_out, up_m_out, up_v_out))
    ins = ((down_ref, down_m_ref, down_v_ref), (up_ref, up_m_ref, up_v_ref))

    def copies(tile):
        columns = pl.ds(pl.multiple_of(tile * UPDATE_TILE, UPDATE_TILE), UPDATE_TILE)
        for side in range(2):
            held = (weights_new.at[side], moments_new.at[side, 0], moments_new.at[side, 1])
            for k in range(3):
                yield pltpu.make_async_copy(
                    held[k].at[:, columns], outs[side][k].at[:, columns], sem.at[side, k]
                )

    @pl.loop(0, WIDTH // UPDATE_TILE)
    def _(tile):
        columns = pl.ds(pl.multiple_of(tile * UPDATE_TILE, UPDATE_TILE), UPDATE_TILE)
        for side in range(2):
            gradient = grad_ref[side * RANK : (side + 1) * RANK, columns].astype(F32)
            if side == 0:
                gradient = gradient * gain_ref[:, columns]
            weight, one, two = ins[side]
            first_new = beta_one * one[:, columns] + (1.0 - beta_one) * gradient
            second_new = beta_two * two[:, columns] + (1.0 - beta_two) * gradient * gradient
            value = weight[:, columns].astype(F32)
            step = (first_new * (1.0 / (1.0 - beta_one**step_count))) * lax.rsqrt(
                second_new * (1.0 / (1.0 - beta_two**step_count)) + eps_root
            )
            weights_new[side, :, columns] = (
                value - learn_rate * (step + decay_rate * value)
            ).astype(BF16)
            moments_new[side, 0, :, columns] = first_new
            moments_new[side, 1, :, columns] = second_new
        for copy in copies(tile):
            copy.start()

    for side in range(2):
        held = (weights_new.at[side], moments_new.at[side, 0], moments_new.at[side, 1])
        for k in range(3):
            pltpu.make_async_copy(held[k], held[k], sem.at[side, k]).wait()


def adamw(grad, gain, down, up, down_m, down_v, up_m, up_v):
    shape = lambda dtype: jax.ShapeDtypeStruct((RANK, WIDTH), dtype)
    whole = pl.BlockSpec(memory_space=pltpu.VMEM)
    anywhere = pl.BlockSpec(memory_space=pl.ANY)
    return pl.pallas_call(
        adamw_kernel,
        in_specs=[whole] * 8,
        out_specs=[anywhere] * 6,
        out_shape=[shape(BF16), shape(BF16), shape(F32), shape(F32), shape(F32), shape(F32)],
        scratch_shapes=[
            pltpu.VMEM((2, RANK, WIDTH), BF16),
            pltpu.VMEM((2, 2, RANK, WIDTH), F32),
            pltpu.SemaphoreType.DMA((2, 3)),
        ],
        compiler_params=pltpu.CompilerParams(vmem_limit_bytes=16 * 2**20),
    )(grad, gain, down, up, down_m, down_v, up_m, up_v)


def body(
    stack_input,
    output_gradient,
    norm_scale_weight,
    row_adapter_index,
    adapter_owner_index,
    adapter_down_weight,
    adapter_up_weight,
    down_first_moment,
    down_second_moment,
    up_first_moment,
    up_second_moment,
):
    down, up, down_m, down_v, up_m, up_v = (
        array.reshape(RANK, WIDTH)
        for array in (
            adapter_down_weight,
            adapter_up_weight,
            down_first_moment,
            down_second_moment,
            up_first_moment,
            up_second_moment,
        )
    )
    grad = gradients(
        stack_input,
        output_gradient,
        norm_scale_weight,
        row_adapter_index.reshape(2, ROWS),
        adapter_owner_index.reshape(1, OWNERS),
        down,
        up,
    )
    results = adamw(grad, norm_scale_weight, down, up, down_m, down_v, up_m, up_v)
    return tuple(array.reshape(1, 1, RANK, WIDTH) for array in results)


def solution(mesh):
    by_owner = P("pipe", "dp", None, None)
    return jax.shard_map(
        body,
        mesh=mesh,
        in_specs=(
            P(None, "dp", "pipe"),
            P(None, "dp", "pipe"),
            P("pipe", None),
            P(None, "dp", None),
            P(),
        )
        + (by_owner,) * 6,
        out_specs=(by_owner,) * 6,
        check_vma=False,
    )
```

```python
import functools

import jax
import jax.numpy as jnp
from jax import lax
from jax.experimental import pallas as pl
from jax.experimental.pallas import tpu as pltpu
from jax.sharding import PartitionSpec as P

adapter_scale = 0.5
beta_one = 0.9
beta_two = 0.999
step_count = 10
learn_rate = 0.001
decay_rate = 0.01
eps_root = 1e-08
eps_norm = 1e-05

MESH = pl.DeviceIdType.MESH
F32 = jnp.float32
BF16 = jnp.bfloat16
RANK = 32
WIDTH = 8192
HALF = 4096
OWNERS = 64
CAP = 4
ROWS = 128
PIECE = 16
GROUPS = 8
MEMBERS = OWNERS // GROUPS
HALF_ROWS = MEMBERS // 2 * PIECE
GROUP_ROWS = MEMBERS * PIECE
SPLIT = 4
PART = HALF // SPLIT
AHEAD = 3
DEFER = 1
TILE = 1024
UPDATE_TILE = 1024


def here():
    pipe, dp = lax.axis_index("pipe"), lax.axis_index("dp")
    core, x_hi = lax.rem(dp, 2), lax.rem(lax.div(dp, 2), 2)
    return pipe, core, x_hi, lax.rem(lax.div(dp, 4), 4) + 4, lax.div(dp, 16) + 4, 1 - 2 * core


def partner_of(place, at):
    pipe, core, x_hi, y, z, sense = at
    member = lax.rem(place, MEMBERS)
    dx = lax.div(member, MEMBERS // 2)
    rank = lax.div(place, MEMBERS) * (MEMBERS // 2) + lax.rem(member, MEMBERS // 2)
    mixed = lax.rem(5 * rank, 16)
    dz = lax.div(mixed, 4)
    dy = 2 * lax.rem(lax.div(mixed, 2), 2) + lax.rem(lax.div(rank, 16) + dx + dz, 2)
    z = lax.rem(z + sense * dz, 4)
    y = lax.rem(y + sense * dy, 4)
    target = z * 16 + y * 4 + lax.rem(x_hi + dx, 2) * 2 + lax.rem(core + mixed, 2)
    return lax.rem(pipe + dx, 2), target


def place_rows(labels_ref, owner_ref):
    lane = lax.broadcasted_iota(jnp.int32, (ROWS, ROWS), 1)
    line = lax.broadcasted_iota(jnp.int32, (ROWS, ROWS), 0)
    owner_row = owner_ref[...].astype(F32)
    parts = []
    for micro in range(2):
        label_row = jnp.broadcast_to(labels_ref[micro : micro + 1, :].astype(F32), (ROWS, ROWS))
        label = label_row.T
        within = jnp.sum(
            jnp.where((label == label_row) & (lane < line), 1.0, 0.0), axis=1, keepdims=True
        )
        target = jnp.sum(
            jnp.where(label[:, :OWNERS] == lane[:, :OWNERS].astype(F32), owner_row, 0.0),
            axis=1,
            keepdims=True,
        )
        slot = jnp.broadcast_to(target * (2 * CAP) + micro * CAP + within, (ROWS, ROWS)).T[:1, :]
        want = lax.broadcasted_iota(jnp.int32, (OWNERS * 2 * CAP, ROWS), 0).astype(F32)
        parts.append(jnp.where(want == slot, 1.0, 0.0))
    return jnp.concatenate(parts, axis=1).astype(BF16)


def row_factors(total_h, total_g, gram):
    dot = functools.partial(jnp.dot, preferred_element_type=F32, precision=lax.Precision.HIGHEST)
    squares = total_h[:, 96:97]
    r0 = lax.rsqrt(squares * (1.0 / WIDTH) + eps_norm)
    low0 = (r0 * total_h[:, 0:32]).astype(BF16).astype(F32)
    moved = dot(low0, gram[32:64, :])
    h1_up0 = total_h[:, 32:64] + adapter_scale * moved[:, 32:64]
    h1_down1 = total_h[:, 64:96] + adapter_scale * moved[:, 64:96]
    squares1 = squares + jnp.sum(
        low0 * (2 * adapter_scale * total_h[:, 32:64] + adapter_scale**2 * moved[:, 32:64]),
        axis=1,
        keepdims=True,
    )
    r1 = lax.rsqrt(jnp.maximum(squares1, 0.0) * (1.0 / WIDTH) + eps_norm)
    low1 = (r1 * h1_down1).astype(BF16).astype(F32)
    lg1 = (adapter_scale * total_g[:, 96:128]).astype(BF16).astype(F32)
    mean = jnp.sum(lg1 * h1_down1, axis=1, keepdims=True) * (1.0 / WIDTH)
    cube = r1 * r1 * r1 * mean
    scaled1 = r1 * lg1
    g1_up0 = total_g[:, 32:64] + dot(scaled1, gram[64:96, :])[:, 32:64] - cube * h1_up0
    lg0 = (adapter_scale * g1_up0).astype(BF16).astype(F32)
    zero = jnp.zeros_like(low0)
    for_h = jnp.concatenate([r0 * lg0, -cube * low0, scaled1, zero], axis=1)
    for_g = jnp.concatenate([zero, low0, zero, low1], axis=1)
    cross_h = jnp.concatenate([zero, low0, zero, zero], axis=1)
    cross_g = jnp.concatenate([zero, zero, scaled1, zero], axis=1)
    return for_h, for_g, cross_h, cross_g


def interleave(upper, lower):
    columns = upper.shape[-1]
    both = jnp.concatenate(
        [upper.reshape(-1, 8, columns), lower.reshape(-1, 8, columns)], axis=1
    )
    return both.astype(BF16)


def gradient_kernel(
    h_hbm,
    g_hbm,
    gain_hbm,
    labels_hbm,
    owner_hbm,
    down_hbm,
    up_hbm,
    grad_ref,
    h_in,
    g_in,
    gain_ref,
    labels_ref,
    owner_ref,
    down_ref,
    up_ref,
    send,
    recv,
    weights,
    products,
    products_in,
    gram,
    total,
    cross,
    grad_out,
    grad_in,
    in_sem,
    send_sem,
    recv_sem,
    weight_sem,
    product_send_sem,
    product_sem,
    grad_sem,
):
    pipe = lax.axis_index("pipe")
    dp = lax.axis_index("dp")
    other = (1 - pipe, dp)

    copies_in = [
        pltpu.make_async_copy(*pair, in_sem.at[n])
        for n, pair in enumerate(
            (
                (labels_hbm, labels_ref),
                (owner_hbm, owner_ref),
                (h_hbm, h_in),
                (g_hbm, g_in),
                (gain_hbm, gain_ref),
                (down_hbm, down_ref),
                (up_hbm, up_ref),
            )
        )
    ]
    for copy in copies_in:
        copy.start()

    barrier = pltpu.get_barrier_semaphore()

    at = here()

    @pl.loop(1, OWNERS)
    def _(i):
        target = lax.rem(dp + i, OWNERS)
        same = 1 - lax.rem(lax.div(target, 2) + at[2], 2)
        pl.semaphore_signal(
            barrier, inc=1, device_id=(lax.rem(pipe + 1 - same, 2), target), device_id_type=MESH
        )

    pl.semaphore_signal(barrier, inc=1, device_id=other, device_id_type=MESH)

    layer = pl.ds(pl.multiple_of(pipe * 2 * RANK, 2 * RANK), 2 * RANK)
    copies_in[0].wait()
    copies_in[1].wait()
    placing = place_rows(labels_ref, owner_ref)
    copies_in[2].wait()
    copies_in[3].wait()

    pl.semaphore_wait(barrier, OWNERS)

    def weight_copy(side, part):
        columns = slice(part * PART, (part + 1) * PART)
        return pltpu.make_async_remote_copy(
            src_ref=weights.at[1 - side, layer, columns],
            dst_ref=weights.at[side, layer, columns],
            send_sem=weight_sem.at[0, side, part],
            recv_sem=weight_sem.at[1, side, part],
            device_id=other,
            device_id_type=MESH,
        )

    def start_part(place, part):
        target = partner_of(place, at)
        columns = pl.ds(pl.multiple_of(part * PART, PART), PART)
        pltpu.make_async_remote_copy(
            src_ref=send.at[target[1], :, columns],
            dst_ref=recv.at[place, :, columns],
            send_sem=send_sem,
            recv_sem=recv_sem.at[lax.div(place, MEMBERS)],
            device_id=target,
            device_id_type=MESH,
        ).start()

    def start_group(group, part, first=0):
        @pl.loop(first, MEMBERS)
        def _(i):
            start_part(
                group * MEMBERS + lax.rem(i, 2) * (MEMBERS // 2) + lax.div(i, 2), part
            )

    def prepare_weights():
        for copy in copies_in[4:]:
            copy.wait()
        for side, half in enumerate((pipe, 1 - pipe)):
            columns = pl.ds(pl.multiple_of(half * HALF, HALF), HALF)
            weights[side, pl.ds(pl.multiple_of(pipe * 2 * RANK, RANK), RANK), :] = (
                down_ref[:, columns].astype(F32) * gain_ref[:, columns]
            ).astype(BF16)
            weights[side, pl.ds(pl.multiple_of(pipe * 2 * RANK + RANK, RANK), RANK), :] = up_ref[
                :, columns
            ]

    for part in range(SPLIT):
        columns = slice(part * PART, (part + 1) * PART)
        packed_h = jnp.dot(
            placing, h_in[:, :, columns].reshape(2 * ROWS, PART), preferred_element_type=F32
        )
        packed_g = jnp.dot(
            placing, g_in[:, :, columns].reshape(2 * ROWS, PART), preferred_element_type=F32
        )
        send[:, :, columns] = interleave(packed_h, packed_g)
        start_group(0, part, 1)
        if part == 0:
            prepare_weights()
        weight_copy(0, part).start()
        weight_copy(1, part).start()

    @pl.loop(1, AHEAD)
    def _(group):
        @pl.loop(0, SPLIT)
        def _(part):
            start_group(group, part)

    copy_self = pltpu.make_async_copy(send.at[dp], recv.at[0], recv_sem.at[0])
    copy_self.start()
    total[...] = jnp.zeros_like(total)
    cross[...] = jnp.zeros_like(cross)

    def start_products(slot):
        pltpu.make_async_remote_copy(
            src_ref=products.at[slot],
            dst_ref=products_in.at[slot],
            send_sem=product_send_sem,
            recv_sem=product_sem.at[slot],
            device_id=other,
            device_id_type=MESH,
        ).start()

    def wait_products(slot):
        pltpu.make_async_copy(
            products_in.at[slot], products_in.at[slot], product_sem.at[slot]
        ).wait()

    for side in range(2):
        for part in range(SPLIT):
            weight_copy(side, part).wait()
    products[GROUPS] = lax.dot_general(
        weights[0], weights[0], (((1,), (1,)), ((), ())), preferred_element_type=F32
    )
    start_products(GROUPS)

    row = lax.broadcasted_iota(jnp.int32, (2 * RANK, TILE), 0)
    scale = jnp.where(row < RANK, 1.0, adapter_scale)

    def mask_cross(side):
        line = lax.broadcasted_iota(jnp.int32, (4 * RANK, 4 * RANK), 0) // RANK
        lane = lax.broadcasted_iota(jnp.int32, (4 * RANK, 4 * RANK), 1) // RANK
        keep = jnp.where((lane == 1) & ((line == 1) | (line == 2)), adapter_scale, 0.0)
        keep = jnp.where((lane == 2) & (line == 1), 1.0, keep)
        cross[side] = cross[side] * keep

    def finish(side, section, columns):
        at = pl.ds(pl.multiple_of(section * 2 * RANK, 2 * RANK), 2 * RANK)
        whole = total[side, at, columns] + jnp.dot(
            cross[side, at, :].astype(BF16),
            weights[side, :, columns],
            preferred_element_type=F32,
        )
        return whole * scale

    def grad_copy(side, tile):
        columns = slice(tile * TILE, (tile + 1) * TILE)
        return pltpu.make_async_remote_copy(
            src_ref=grad_out.at[side, :, columns],
            dst_ref=grad_in.at[side, :, columns],
            send_sem=grad_sem.at[0, side, tile],
            recv_sem=grad_sem.at[1, side, tile],
            device_id=other,
            device_id_type=MESH,
        )

    def hand_over(side):
        mask_cross(side)
        for tile in range(HALF // TILE):
            columns = slice(tile * TILE, (tile + 1) * TILE)
            grad_out[side, :, columns] = finish(side, 1 - pipe, columns).astype(BF16)
            grad_copy(side, tile).start()

    by_rows = (((1,), (1,)), ((), ()))
    over_rows = (((0,), (0,)), ((), ()))

    @pl.loop(0, GROUPS + DEFER)
    def _(group):
        @pl.when(group < GROUPS)
        def _():
            first = group * MEMBERS
            members = pl.ds(first, MEMBERS)
            pltpu.make_async_copy(recv.at[members], recv.at[members], recv_sem.at[group]).wait()
            halves = [
                (pl.ds(first, MEMBERS // 2), 0),
                (pl.ds(first + MEMBERS // 2, MEMBERS // 2), 1),
            ]
            product = [jnp.zeros((HALF_ROWS, 4 * RANK), F32) for _ in halves]
            squares = [jnp.zeros((HALF_ROWS, ROWS), F32) for _ in halves]
            for tile in range(HALF // TILE):
                columns = slice(tile * TILE, (tile + 1) * TILE)
                for n, (half, side) in enumerate(halves):
                    rows = recv[half, :, columns].reshape(HALF_ROWS, TILE)
                    product[n] += lax.dot_general(
                        rows, weights[side, :, columns], by_rows, preferred_element_type=F32
                    )
                    wide = rows.astype(F32)
                    for k in range(TILE // ROWS):
                        piece = wide[:, k * ROWS : (k + 1) * ROWS]
                        squares[n] += piece * piece
            product = jnp.concatenate(product, axis=0)
            squares = jnp.sum(jnp.concatenate(squares, axis=0), axis=1, keepdims=True)
            line = lax.broadcasted_iota(jnp.int32, product.shape, 0) % PIECE
            lane = lax.broadcasted_iota(jnp.int32, product.shape, 1)
            products[group] = jnp.where((line < 8) & (lane >= 3 * RANK), squares, product)
            start_products(group)

            @pl.when(group + AHEAD < GROUPS)
            def _():
                @pl.loop(0, SPLIT)
                def _(part):
                    start_group(group + AHEAD, part)

        @pl.when(group == DEFER)
        def _():
            wait_products(GROUPS)
            gram[...] = products[GROUPS] + products_in[GROUPS]

        @pl.when(group >= DEFER)
        def _():
            done = group - DEFER
            wait_products(done)
            both = (products[done] + products_in[done]).reshape(MEMBERS, PIECE, 4 * RANK)
            for_h, for_g, cross_h, cross_g = row_factors(
                both[:, :8, :].reshape(-1, 4 * RANK), both[:, 8:, :].reshape(-1, 4 * RANK), gram[...]
            )
            factors = interleave(for_h, for_g).reshape(GROUP_ROWS, 4 * RANK)
            beside = interleave(cross_h, cross_g).reshape(GROUP_ROWS, 4 * RANK)
            first = done * MEMBERS

            def add(rows_at, picked, side):
                cross[side] += lax.dot_general(
                    factors[picked], beside[picked], over_rows, preferred_element_type=F32
                )
                for tile in range(HALF // TILE):
                    columns = slice(tile * TILE, (tile + 1) * TILE)
                    rows = recv[rows_at, :, columns].reshape(-1, TILE)
                    total[side, :, columns] += lax.dot_general(
                        factors[picked], rows, over_rows, preferred_element_type=F32
                    )

            add(pl.ds(first, MEMBERS // 2), slice(0, HALF_ROWS), 0)
            add(pl.ds(first + MEMBERS // 2, MEMBERS // 2), slice(HALF_ROWS, None), 1)

    hand_over(1)
    hand_over(0)
    for side, half in enumerate((pipe, 1 - pipe)):
        for tile in range(HALF // TILE):
            columns = slice(tile * TILE, (tile + 1) * TILE)
            mine = finish(side, pipe, columns)
            grad_copy(1 - side, tile).wait()
            at = pl.ds(pl.multiple_of(half * HALF + tile * TILE, TILE), TILE)
            grad_ref[:, at] = mine + grad_in[1 - side, :, columns].astype(F32)
    pltpu.make_async_copy(send.at[pl.ds(1, 63)], send.at[pl.ds(1, 63)], send_sem).wait()
    pltpu.make_async_copy(products, products, product_send_sem).wait()


def gradients(stack_input, output_gradient, gain, labels, owners, down, up):
    whole = pl.BlockSpec(memory_space=pltpu.VMEM)
    return pl.pallas_call(
        gradient_kernel,
        out_shape=jax.ShapeDtypeStruct((2 * RANK, WIDTH), F32),
        in_specs=[pl.BlockSpec(memory_space=pl.ANY)] * 7,
        out_specs=whole,
        scratch_shapes=[
            pltpu.VMEM((2, ROWS, HALF), BF16),
            pltpu.VMEM((2, ROWS, HALF), BF16),
            pltpu.VMEM((1, WIDTH), F32),
            pltpu.VMEM((2, ROWS), jnp.int32),
            pltpu.VMEM((1, OWNERS), jnp.int32),
            pltpu.VMEM((RANK, WIDTH), BF16),
            pltpu.VMEM((RANK, WIDTH), BF16),
            pltpu.VMEM((OWNERS, PIECE, HALF), BF16),
            pltpu.VMEM((OWNERS, PIECE, HALF), BF16),
            pltpu.VMEM((2, 4 * RANK, HALF), BF16),
            pltpu.VMEM((GROUPS + 1, GROUP_ROWS, 4 * RANK), F32),
            pltpu.VMEM((GROUPS + 1, GROUP_ROWS, 4 * RANK), F32),
            pltpu.VMEM((4 * RANK, 4 * RANK), F32),
            pltpu.VMEM((2, 4 * RANK, HALF), F32),
            pltpu.VMEM((2, 4 * RANK, 4 * RANK), F32),
            pltpu.VMEM((2, 2 * RANK, HALF), BF16),
            pltpu.VMEM((2, 2 * RANK, HALF), BF16),
            pltpu.SemaphoreType.DMA((7,)),
            pltpu.SemaphoreType.DMA(()),
            pltpu.SemaphoreType.DMA((GROUPS,)),
            pltpu.SemaphoreType.DMA((2, 2, SPLIT)),
            pltpu.SemaphoreType.DMA(()),
            pltpu.SemaphoreType.DMA((GROUPS + 1,)),
            pltpu.SemaphoreType.DMA((2, 2, HALF // TILE)),
        ],
        compiler_params=pltpu.CompilerParams(
            collective_id=0, has_side_effects=True, vmem_limit_bytes=56 * 2**20
        ),
    )(stack_input, output_gradient, gain, labels, owners, down, up)


def adamw_kernel(
    grad_ref,
    gain_ref,
    down_ref,
    up_ref,
    down_m_ref,
    down_v_ref,
    up_m_ref,
    up_v_ref,
    down_out,
    up_out,
    down_m_out,
    down_v_out,
    up_m_out,
    up_v_out,
    weights_new,
    moments_new,
    sem,
):
    outs = ((down_out, down_m_out, down_v_out), (up_out, up_m_out, up_v_out))
    ins = ((down_ref, down_m_ref, down_v_ref), (up_ref, up_m_ref, up_v_ref))

    def copies(tile):
        columns = pl.ds(pl.multiple_of(tile * UPDATE_TILE, UPDATE_TILE), UPDATE_TILE)
        for side in range(2):
            held = (weights_new.at[side], moments_new.at[side, 0], moments_new.at[side, 1])
            for k in range(3):
                yield pltpu.make_async_copy(
                    held[k].at[:, columns], outs[side][k].at[:, columns], sem.at[side, k]
                )

    @pl.loop(0, WIDTH // UPDATE_TILE)
    def _(tile):
        columns = pl.ds(pl.multiple_of(tile * UPDATE_TILE, UPDATE_TILE), UPDATE_TILE)
        for side in range(2):
            gradient = grad_ref[side * RANK : (side + 1) * RANK, columns].astype(F32)
            if side == 0:
                gradient = gradient * gain_ref[:, columns]
            weight, one, two = ins[side]
            first_new = beta_one * one[:, columns] + (1.0 - beta_one) * gradient
            second_new = beta_two * two[:, columns] + (1.0 - beta_two) * gradient * gradient
            value = weight[:, columns].astype(F32)
            step = (first_new * (1.0 / (1.0 - beta_one**step_count))) * lax.rsqrt(
                second_new * (1.0 / (1.0 - beta_two**step_count)) + eps_root
            )
            weights_new[side, :, columns] = (
                value - learn_rate * (step + decay_rate * value)
            ).astype(BF16)
            moments_new[side, 0, :, columns] = first_new
            moments_new[side, 1, :, columns] = second_new
        for copy in copies(tile):
            copy.start()

    for side in range(2):
        held = (weights_new.at[side], moments_new.at[side, 0], moments_new.at[side, 1])
        for k in range(3):
            pltpu.make_async_copy(held[k], held[k], sem.at[side, k]).wait()


def adamw(grad, gain, down, up, down_m, down_v, up_m, up_v):
    shape = lambda dtype: jax.ShapeDtypeStruct((RANK, WIDTH), dtype)
    whole = pl.BlockSpec(memory_space=pltpu.VMEM)
    anywhere = pl.BlockSpec(memory_space=pl.ANY)
    return pl.pallas_call(
        adamw_kernel,
        in_specs=[whole] * 8,
        out_specs=[anywhere] * 6,
        out_shape=[shape(BF16), shape(BF16), shape(F32), shape(F32), shape(F32), shape(F32)],
        scratch_shapes=[
            pltpu.VMEM((2, RANK, WIDTH), BF16),
            pltpu.VMEM((2, 2, RANK, WIDTH), F32),
            pltpu.SemaphoreType.DMA((2, 3)),
        ],
        compiler_params=pltpu.CompilerParams(vmem_limit_bytes=16 * 2**20),
    )(grad, gain, down, up, down_m, down_v, up_m, up_v)


def body(
    stack_input,
    output_gradient,
    norm_scale_weight,
    row_adapter_index,
    adapter_owner_index,
    adapter_down_weight,
    adapter_up_weight,
    down_first_moment,
    down_second_moment,
    up_first_moment,
    up_second_moment,
):
    down, up, down_m, down_v, up_m, up_v = (
        array.reshape(RANK, WIDTH)
        for array in (
            adapter_down_weight,
            adapter_up_weight,
            down_first_moment,
            down_second_moment,
            up_first_moment,
            up_second_moment,
        )
    )
    grad = gradients(
        stack_input,
        output_gradient,
        norm_scale_weight,
        row_adapter_index.reshape(2, ROWS),
        adapter_owner_index.reshape(1, OWNERS),
        down,
        up,
    )
    results = adamw(grad, norm_scale_weight, down, up, down_m, down_v, up_m, up_v)
    return tuple(array.reshape(1, 1, RANK, WIDTH) for array in results)


def solution(mesh):
    by_owner = P("pipe", "dp", None, None)
    return jax.shard_map(
        body,
        mesh=mesh,
        in_specs=(
            P(None, "dp", "pipe"),
            P(None, "dp", "pipe"),
            P("pipe", None),
            P(None, "dp", None),
            P(),
        )
        + (by_owner,) * 6,
        out_specs=(by_owner,) * 6,
        check_vma=False,
    )
```

```python
import functools

import jax
import jax.numpy as jnp
from jax import lax
from jax.experimental import pallas as pl
from jax.experimental.pallas import tpu as pltpu
from jax.sharding import PartitionSpec as P

adapter_scale = 0.5
beta_one = 0.9
beta_two = 0.999
step_count = 10
learn_rate = 0.001
decay_rate = 0.01
eps_root = 1e-08
eps_norm = 1e-05

MESH = pl.DeviceIdType.MESH
F32 = jnp.float32
BF16 = jnp.bfloat16
RANK = 32
WIDTH = 8192
HALF = 4096
OWNERS = 64
CAP = 4
ROWS = 128
PIECE = 16
GROUPS = 8
MEMBERS = OWNERS // GROUPS
HALF_ROWS = MEMBERS // 2 * PIECE
GROUP_ROWS = MEMBERS * PIECE
SPLIT = 4
PART = HALF // SPLIT
AHEAD = 3
TILE = 1024
UPDATE_TILE = 1024


def here():
    pipe, dp = lax.axis_index("pipe"), lax.axis_index("dp")
    core, x_hi = lax.rem(dp, 2), lax.rem(lax.div(dp, 2), 2)
    return pipe, core, x_hi, lax.rem(lax.div(dp, 4), 4) + 4, lax.div(dp, 16) + 4, 1 - 2 * core


def partner_of(place, at):
    pipe, core, x_hi, y, z, sense = at
    member = lax.rem(place, MEMBERS)
    dx = lax.div(member, MEMBERS // 2)
    rank = lax.div(place, MEMBERS) * (MEMBERS // 2) + lax.rem(member, MEMBERS // 2)
    mixed = lax.rem(5 * rank, 16)
    dz = lax.div(mixed, 4)
    dy = 2 * lax.rem(lax.div(mixed, 2), 2) + lax.rem(lax.div(rank, 16) + dx + dz, 2)
    z = lax.rem(z + sense * dz, 4)
    y = lax.rem(y + sense * dy, 4)
    target = z * 16 + y * 4 + lax.rem(x_hi + dx, 2) * 2 + lax.rem(core + mixed, 2)
    return lax.rem(pipe + dx, 2), target


def place_rows(labels_ref, owner_ref):
    lane = lax.broadcasted_iota(jnp.int32, (ROWS, ROWS), 1)
    line = lax.broadcasted_iota(jnp.int32, (ROWS, ROWS), 0)
    owner_row = owner_ref[...].astype(F32)
    parts = []
    for micro in range(2):
        label_row = jnp.broadcast_to(labels_ref[micro : micro + 1, :].astype(F32), (ROWS, ROWS))
        label = label_row.T
        within = jnp.sum(
            jnp.where((label == label_row) & (lane < line), 1.0, 0.0), axis=1, keepdims=True
        )
        target = jnp.sum(
            jnp.where(label[:, :OWNERS] == lane[:, :OWNERS].astype(F32), owner_row, 0.0),
            axis=1,
            keepdims=True,
        )
        slot = jnp.broadcast_to(target * (2 * CAP) + micro * CAP + within, (ROWS, ROWS)).T[:1, :]
        want = lax.broadcasted_iota(jnp.int32, (OWNERS * 2 * CAP, ROWS), 0).astype(F32)
        parts.append(jnp.where(want == slot, 1.0, 0.0))
    return jnp.concatenate(parts, axis=1).astype(BF16)


def row_factors(total_h, total_g, gram):
    dot = functools.partial(jnp.dot, preferred_element_type=F32, precision=lax.Precision.HIGHEST)
    squares = total_h[:, 96:97]
    r0 = lax.rsqrt(squares * (1.0 / WIDTH) + eps_norm)
    low0 = (r0 * total_h[:, 0:32]).astype(BF16).astype(F32)
    moved = dot(low0, gram[32:64, :])
    h1_up0 = total_h[:, 32:64] + adapter_scale * moved[:, 32:64]
    h1_down1 = total_h[:, 64:96] + adapter_scale * moved[:, 64:96]
    squares1 = squares + jnp.sum(
        low0 * (2 * adapter_scale * total_h[:, 32:64] + adapter_scale**2 * moved[:, 32:64]),
        axis=1,
        keepdims=True,
    )
    r1 = lax.rsqrt(jnp.maximum(squares1, 0.0) * (1.0 / WIDTH) + eps_norm)
    low1 = (r1 * h1_down1).astype(BF16).astype(F32)
    lg1 = (adapter_scale * total_g[:, 96:128]).astype(BF16).astype(F32)
    mean = jnp.sum(lg1 * h1_down1, axis=1, keepdims=True) * (1.0 / WIDTH)
    cube = r1 * r1 * r1 * mean
    scaled1 = r1 * lg1
    g1_up0 = total_g[:, 32:64] + dot(scaled1, gram[64:96, :])[:, 32:64] - cube * h1_up0
    lg0 = (adapter_scale * g1_up0).astype(BF16).astype(F32)
    zero = jnp.zeros_like(low0)
    for_h = jnp.concatenate([r0 * lg0, -cube * low0, scaled1, zero], axis=1)
    for_g = jnp.concatenate([zero, low0, zero, low1], axis=1)
    cross_h = jnp.concatenate([zero, low0, zero, zero], axis=1)
    cross_g = jnp.concatenate([zero, zero, scaled1, zero], axis=1)
    return for_h, for_g, cross_h, cross_g


def interleave(upper, lower):
    columns = upper.shape[-1]
    both = jnp.concatenate(
        [upper.reshape(-1, 8, columns), lower.reshape(-1, 8, columns)], axis=1
    )
    return both.astype(BF16)


def gradient_kernel(
    h_hbm,
    g_hbm,
    gain_hbm,
    labels_hbm,
    owner_hbm,
    down_hbm,
    up_hbm,
    grad_hbm,
    h_in,
    g_in,
    gain_ref,
    labels_ref,
    owner_ref,
    down_ref,
    up_ref,
    send,
    recv,
    weights,
    products,
    products_in,
    gram,
    total,
    cross,
    grad_out,
    grad_in,
    grad_whole,
    in_sem,
    send_sem,
    recv_sem,
    weight_sem,
    product_send_sem,
    product_sem,
    grad_sem,
    out_sem,
):
    pipe = lax.axis_index("pipe")
    dp = lax.axis_index("dp")
    other = (1 - pipe, dp)

    copies_in = [
        pltpu.make_async_copy(*pair, in_sem.at[n])
        for n, pair in enumerate(
            (
                (labels_hbm, labels_ref),
                (owner_hbm, owner_ref),
                (h_hbm, h_in),
                (g_hbm, g_in),
                (gain_hbm, gain_ref),
                (down_hbm, down_ref),
                (up_hbm, up_ref),
            )
        )
    ]
    for copy in copies_in:
        copy.start()

    barrier = pltpu.get_barrier_semaphore()

    at = here()

    @pl.loop(1, OWNERS)
    def _(i):
        target = lax.rem(dp + i, OWNERS)
        same = 1 - lax.rem(lax.div(target, 2) + at[2], 2)
        pl.semaphore_signal(
            barrier, inc=1, device_id=(lax.rem(pipe + 1 - same, 2), target), device_id_type=MESH
        )

    pl.semaphore_signal(barrier, inc=1, device_id=other, device_id_type=MESH)

    layer = pl.ds(pl.multiple_of(pipe * 2 * RANK, 2 * RANK), 2 * RANK)
    copies_in[0].wait()
    copies_in[1].wait()
    placing = place_rows(labels_ref, owner_ref)
    copies_in[2].wait()
    copies_in[3].wait()

    pl.semaphore_wait(barrier, OWNERS)

    def weight_copy(side, part):
        columns = slice(part * PART, (part + 1) * PART)
        return pltpu.make_async_remote_copy(
            src_ref=weights.at[1 - side, layer, columns],
            dst_ref=weights.at[side, layer, columns],
            send_sem=weight_sem.at[0, side, part],
            recv_sem=weight_sem.at[1, side, part],
            device_id=other,
            device_id_type=MESH,
        )

    def start_part(place, part):
        target = partner_of(place, at)
        columns = pl.ds(pl.multiple_of(part * PART, PART), PART)
        pltpu.make_async_remote_copy(
            src_ref=send.at[target[1], :, columns],
            dst_ref=recv.at[place, :, columns],
            send_sem=send_sem,
            recv_sem=recv_sem.at[lax.div(place, MEMBERS)],
            device_id=target,
            device_id_type=MESH,
        ).start()

    def start_group(group, part, first=0):
        @pl.loop(first, MEMBERS)
        def _(i):
            start_part(
                group * MEMBERS + lax.rem(i, 2) * (MEMBERS // 2) + lax.div(i, 2), part
            )

    def prepare_weights():
        for copy in copies_in[4:]:
            copy.wait()
        for side, half in enumerate((pipe, 1 - pipe)):
            columns = pl.ds(pl.multiple_of(half * HALF, HALF), HALF)
            weights[side, pl.ds(pl.multiple_of(pipe * 2 * RANK, RANK), RANK), :] = (
                down_ref[:, columns].astype(F32) * gain_ref[:, columns]
            ).astype(BF16)
            weights[side, pl.ds(pl.multiple_of(pipe * 2 * RANK + RANK, RANK), RANK), :] = up_ref[
                :, columns
            ]

    for part in range(SPLIT):
        columns = slice(part * PART, (part + 1) * PART)
        packed_h = jnp.dot(
            placing, h_in[:, :, columns].reshape(2 * ROWS, PART), preferred_element_type=F32
        )
        packed_g = jnp.dot(
            placing, g_in[:, :, columns].reshape(2 * ROWS, PART), preferred_element_type=F32
        )
        send[:, :, columns] = interleave(packed_h, packed_g)
        start_group(0, part, 1)
        if part == 0:
            prepare_weights()
        weight_copy(0, part).start()
        weight_copy(1, part).start()

    @pl.loop(1, AHEAD)
    def _(group):
        @pl.loop(0, SPLIT)
        def _(part):
            start_group(group, part)

    copy_self = pltpu.make_async_copy(send.at[dp], recv.at[0], recv_sem.at[0])
    copy_self.start()
    total[...] = jnp.zeros_like(total)
    cross[...] = jnp.zeros_like(cross)

    def start_products(slot):
        pltpu.make_async_remote_copy(
            src_ref=products.at[slot],
            dst_ref=products_in.at[slot],
            send_sem=product_send_sem,
            recv_sem=product_sem.at[slot],
            device_id=other,
            device_id_type=MESH,
        ).start()

    def wait_products(slot):
        pltpu.make_async_copy(
            products_in.at[slot], products_in.at[slot], product_sem.at[slot]
        ).wait()

    for side in range(2):
        for part in range(SPLIT):
            weight_copy(side, part).wait()
    products[GROUPS] = lax.dot_general(
        weights[0], weights[0], (((1,), (1,)), ((), ())), preferred_element_type=F32
    )
    start_products(GROUPS)

    row = lax.broadcasted_iota(jnp.int32, (2 * RANK, TILE), 0)
    scale = jnp.where(row < RANK, 1.0, adapter_scale)

    def mask_cross(side):
        line = lax.broadcasted_iota(jnp.int32, (4 * RANK, 4 * RANK), 0) // RANK
        lane = lax.broadcasted_iota(jnp.int32, (4 * RANK, 4 * RANK), 1) // RANK
        keep = jnp.where((lane == 1) & ((line == 1) | (line == 2)), adapter_scale, 0.0)
        keep = jnp.where((lane == 2) & (line == 1), 1.0, keep)
        cross[side] = cross[side] * keep

    def finish(side, section, columns):
        at = pl.ds(pl.multiple_of(section * 2 * RANK, 2 * RANK), 2 * RANK)
        whole = total[side, at, columns] + jnp.dot(
            cross[side, at, :].astype(BF16),
            weights[side, :, columns],
            preferred_element_type=F32,
        )
        return whole * scale

    def grad_copy(side, tile):
        columns = slice(tile * TILE, (tile + 1) * TILE)
        return pltpu.make_async_remote_copy(
            src_ref=grad_out.at[side, :, columns],
            dst_ref=grad_in.at[side, :, columns],
            send_sem=grad_sem.at[0, side, tile],
            recv_sem=grad_sem.at[1, side, tile],
            device_id=other,
            device_id_type=MESH,
        )

    def hand_over(side):
        mask_cross(side)
        for tile in range(HALF // TILE):
            columns = slice(tile * TILE, (tile + 1) * TILE)
            grad_out[side, :, columns] = finish(side, 1 - pipe, columns).astype(BF16)
            grad_copy(side, tile).start()

    by_rows = (((1,), (1,)), ((), ()))
    over_rows = (((0,), (0,)), ((), ()))

    def use_factors(done, finished):
        wait_products(done)
        both = (products[done] + products_in[done]).reshape(MEMBERS, PIECE, 4 * RANK)
        for_h, for_g, cross_h, cross_g = row_factors(
            both[:, :8, :].reshape(-1, 4 * RANK), both[:, 8:, :].reshape(-1, 4 * RANK), gram[...]
        )
        factors = interleave(for_h, for_g).reshape(GROUP_ROWS, 4 * RANK)
        beside = interleave(cross_h, cross_g).reshape(GROUP_ROWS, 4 * RANK)
        first = done * MEMBERS

        def add(rows_at, picked, side):
            cross[side] += lax.dot_general(
                factors[picked], beside[picked], over_rows, preferred_element_type=F32
            )
            for tile in range(HALF // TILE):
                columns = slice(tile * TILE, (tile + 1) * TILE)
                rows = recv[rows_at, :, columns].reshape(-1, TILE)
                total[side, :, columns] += lax.dot_general(
                    factors[picked], rows, over_rows, preferred_element_type=F32
                )

        add(pl.ds(first + MEMBERS // 2, MEMBERS // 2), slice(HALF_ROWS, None), 1)
        if finished:
            hand_over(1)
        add(pl.ds(first, MEMBERS // 2), slice(0, HALF_ROWS), 0)
        if finished:
            hand_over(0)

    @pl.loop(0, GROUPS)
    def _(group):
        first = group * MEMBERS
        members = pl.ds(first, MEMBERS)
        pltpu.make_async_copy(recv.at[members], recv.at[members], recv_sem.at[group]).wait()
        halves = [
            (pl.ds(first, MEMBERS // 2), 0),
            (pl.ds(first + MEMBERS // 2, MEMBERS // 2), 1),
        ]
        product = [jnp.zeros((HALF_ROWS, 4 * RANK), F32) for _ in halves]
        squares = [jnp.zeros((HALF_ROWS, ROWS), F32) for _ in halves]
        for tile in range(HALF // TILE):
            columns = slice(tile * TILE, (tile + 1) * TILE)
            for n, (half, side) in enumerate(halves):
                rows = recv[half, :, columns].reshape(HALF_ROWS, TILE)
                product[n] += lax.dot_general(
                    rows, weights[side, :, columns], by_rows, preferred_element_type=F32
                )
                wide = rows.astype(F32)
                for k in range(TILE // ROWS):
                    piece = wide[:, k * ROWS : (k + 1) * ROWS]
                    squares[n] += piece * piece
        product = jnp.concatenate(product, axis=0)
        squares = jnp.sum(jnp.concatenate(squares, axis=0), axis=1, keepdims=True)
        line = lax.broadcasted_iota(jnp.int32, product.shape, 0) % PIECE
        lane = lax.broadcasted_iota(jnp.int32, product.shape, 1)
        products[group] = jnp.where((line < 8) & (lane >= 3 * RANK), squares, product)
        start_products(group)

        @pl.when(group + AHEAD < GROUPS)
        def _():
            @pl.loop(0, SPLIT)
            def _(part):
                start_group(group + AHEAD, part)

        @pl.when(group == 1)
        def _():
            wait_products(GROUPS)
            gram[...] = products[GROUPS] + products_in[GROUPS]

        @pl.when(group >= 1)
        def _():
            use_factors(group - 1, False)

    use_factors(GROUPS - 1, True)
    copies_out = []
    for side, half in enumerate((pipe, 1 - pipe)):
        for tile in range(HALF // TILE):
            columns = slice(tile * TILE, (tile + 1) * TILE)
            mine = finish(side, pipe, columns)
            grad_copy(1 - side, tile).wait()
            at = pl.ds(pl.multiple_of(half * HALF + tile * TILE, TILE), TILE)
            grad_whole[side, :, columns] = mine + grad_in[1 - side, :, columns].astype(F32)
            copy = pltpu.make_async_copy(
                grad_whole.at[side, :, columns], grad_hbm.at[:, at], out_sem.at[side, tile]
            )
            copy.start()
            copies_out.append(copy)
    pltpu.make_async_copy(send.at[pl.ds(1, 63)], send.at[pl.ds(1, 63)], send_sem).wait()
    pltpu.make_async_copy(products, products, product_send_sem).wait()
    for copy in copies_out:
        copy.wait()


def gradients(stack_input, output_gradient, gain, labels, owners, down, up):
    return pl.pallas_call(
        gradient_kernel,
        out_shape=jax.ShapeDtypeStruct((2 * RANK, WIDTH), F32),
        in_specs=[pl.BlockSpec(memory_space=pl.ANY)] * 7,
        out_specs=pl.BlockSpec(memory_space=pl.ANY),
        scratch_shapes=[
            pltpu.VMEM((2, ROWS, HALF), BF16),
            pltpu.VMEM((2, ROWS, HALF), BF16),
            pltpu.VMEM((1, WIDTH), F32),
            pltpu.VMEM((2, ROWS), jnp.int32),
            pltpu.VMEM((1, OWNERS), jnp.int32),
            pltpu.VMEM((RANK, WIDTH), BF16),
            pltpu.VMEM((RANK, WIDTH), BF16),
            pltpu.VMEM((OWNERS, PIECE, HALF), BF16),
            pltpu.VMEM((OWNERS, PIECE, HALF), BF16),
            pltpu.VMEM((2, 4 * RANK, HALF), BF16),
            pltpu.VMEM((GROUPS + 1, GROUP_ROWS, 4 * RANK), F32),
            pltpu.VMEM((GROUPS + 1, GROUP_ROWS, 4 * RANK), F32),
            pltpu.VMEM((4 * RANK, 4 * RANK), F32),
            pltpu.VMEM((2, 4 * RANK, HALF), F32),
            pltpu.VMEM((2, 4 * RANK, 4 * RANK), F32),
            pltpu.VMEM((2, 2 * RANK, HALF), BF16),
            pltpu.VMEM((2, 2 * RANK, HALF), BF16),
            pltpu.VMEM((2, 2 * RANK, HALF), F32),
            pltpu.SemaphoreType.DMA((7,)),
            pltpu.SemaphoreType.DMA(()),
            pltpu.SemaphoreType.DMA((GROUPS,)),
            pltpu.SemaphoreType.DMA((2, 2, SPLIT)),
            pltpu.SemaphoreType.DMA(()),
            pltpu.SemaphoreType.DMA((GROUPS + 1,)),
            pltpu.SemaphoreType.DMA((2, 2, HALF // TILE)),
            pltpu.SemaphoreType.DMA((2, HALF // TILE)),
        ],
        compiler_params=pltpu.CompilerParams(
            collective_id=0, has_side_effects=True, vmem_limit_bytes=56 * 2**20
        ),
    )(stack_input, output_gradient, gain, labels, owners, down, up)


def adamw_kernel(
    grad_hbm,
    gain_ref,
    down_ref,
    up_ref,
    down_m_ref,
    down_v_ref,
    up_m_ref,
    up_v_ref,
    down_out,
    up_out,
    down_m_out,
    down_v_out,
    up_m_out,
    up_v_out,
    weights_new,
    moments_new,
    grad_ref,
    sem,
    in_sem,
):
    outs = ((down_out, down_m_out, down_v_out), (up_out, up_m_out, up_v_out))
    ins = ((down_ref, down_m_ref, down_v_ref), (up_ref, up_m_ref, up_v_ref))

    def copies(tile):
        columns = pl.ds(pl.multiple_of(tile * UPDATE_TILE, UPDATE_TILE), UPDATE_TILE)
        for side in range(2):
            held = (weights_new.at[side], moments_new.at[side, 0], moments_new.at[side, 1])
            for k in range(3):
                yield pltpu.make_async_copy(
                    held[k].at[:, columns], outs[side][k].at[:, columns], sem.at[side, k]
                )

    def grad_in(tile):
        columns = pl.ds(pl.multiple_of(tile * UPDATE_TILE, UPDATE_TILE), UPDATE_TILE)
        return pltpu.make_async_copy(
            grad_hbm.at[:, columns], grad_ref.at[:, columns], in_sem.at[tile]
        )

    @pl.loop(0, WIDTH // UPDATE_TILE)
    def _(tile):
        grad_in(tile).start()

    @pl.loop(0, WIDTH // UPDATE_TILE)
    def _(tile):
        columns = pl.ds(pl.multiple_of(tile * UPDATE_TILE, UPDATE_TILE), UPDATE_TILE)
        grad_in(tile).wait()
        for side in range(2):
            gradient = grad_ref[side * RANK : (side + 1) * RANK, columns].astype(F32)
            if side == 0:
                gradient = gradient * gain_ref[:, columns]
            weight, one, two = ins[side]
            first_new = beta_one * one[:, columns] + (1.0 - beta_one) * gradient
            second_new = beta_two * two[:, columns] + (1.0 - beta_two) * gradient * gradient
            value = weight[:, columns].astype(F32)
            step = (first_new * (1.0 / (1.0 - beta_one**step_count))) * lax.rsqrt(
                second_new * (1.0 / (1.0 - beta_two**step_count)) + eps_root
            )
            weights_new[side, :, columns] = (
                value - learn_rate * (step + decay_rate * value)
            ).astype(BF16)
            moments_new[side, 0, :, columns] = first_new
            moments_new[side, 1, :, columns] = second_new
        for copy in copies(tile):
            copy.start()

    for side in range(2):
        held = (weights_new.at[side], moments_new.at[side, 0], moments_new.at[side, 1])
        for k in range(3):
            pltpu.make_async_copy(held[k], held[k], sem.at[side, k]).wait()


def adamw(grad, gain, down, up, down_m, down_v, up_m, up_v):
    shape = lambda dtype: jax.ShapeDtypeStruct((RANK, WIDTH), dtype)
    whole = pl.BlockSpec(memory_space=pltpu.VMEM)
    anywhere = pl.BlockSpec(memory_space=pl.ANY)
    return pl.pallas_call(
        adamw_kernel,
        in_specs=[anywhere] + [whole] * 7,
        out_specs=[anywhere] * 6,
        out_shape=[shape(BF16), shape(BF16), shape(F32), shape(F32), shape(F32), shape(F32)],
        scratch_shapes=[
            pltpu.VMEM((2, RANK, WIDTH), BF16),
            pltpu.VMEM((2, 2, RANK, WIDTH), F32),
            pltpu.VMEM((2 * RANK, WIDTH), F32),
            pltpu.SemaphoreType.DMA((2, 3)),
            pltpu.SemaphoreType.DMA((WIDTH // UPDATE_TILE,)),
        ],
        compiler_params=pltpu.CompilerParams(vmem_limit_bytes=48 * 2**20),
    )(grad, gain, down, up, down_m, down_v, up_m, up_v)


def body(
    stack_input,
    output_gradient,
    norm_scale_weight,
    row_adapter_index,
    adapter_owner_index,
    adapter_down_weight,
    adapter_up_weight,
    down_first_moment,
    down_second_moment,
    up_first_moment,
    up_second_moment,
):
    down, up, down_m, down_v, up_m, up_v = (
        array.reshape(RANK, WIDTH)
        for array in (
            adapter_down_weight,
            adapter_up_weight,
            down_first_moment,
            down_second_moment,
            up_first_moment,
            up_second_moment,
        )
    )
    grad = gradients(
        stack_input,
        output_gradient,
        norm_scale_weight,
        row_adapter_index.reshape(2, ROWS),
        adapter_owner_index.reshape(1, OWNERS),
        down,
        up,
    )
    results = adamw(grad, norm_scale_weight, down, up, down_m, down_v, up_m, up_v)
    return tuple(array.reshape(1, 1, RANK, WIDTH) for array in results)


def solution(mesh):
    by_owner = P("pipe", "dp", None, None)
    return jax.shard_map(
        body,
        mesh=mesh,
        in_specs=(
            P(None, "dp", "pipe"),
            P(None, "dp", "pipe"),
            P("pipe", None),
            P(None, "dp", None),
            P(),
        )
        + (by_owner,) * 6,
        out_specs=(by_owner,) * 6,
        check_vma=False,
    )
```
